32 devices in a mesh: section: 2 (over x), tensor: 2 (over core), fsdp: 8 (over z, y).
Axes of the slice: x: 2, y: 2, z: 4, core: 2. Of those that a mesh axis runs over, the one named last changes fastest.
Arguments:
- tokens: bfloat16 [2, 16, 82, 384], P(None, ('fsdp', 'tensor')), may hold values from -6 to 6
- out_grad: bfloat16 [2, 16, 82, 384], P(None, ('fsdp', 'tensor')), may hold values from -6 to 6
- image_count: int32 [2, 8], P(None, 'fsdp'), may hold values from 1 to 2, as said below
- w_qkv: bfloat16 [2, 384, 3, 384], P('section', 'fsdp', None, 'tensor'), may hold values from -0.3125 to 0.3125
- w_out: bfloat16 [2, 384, 384], P('section', 'tensor', 'fsdp'), may hold values from -1.25 to 1.25
- w_up: bfloat16 [2, 384, 1536], P('section', 'fsdp', 'tensor'), may hold values from -0.3125 to 0.3125
- w_down: bfloat16 [2, 1536, 384], P('section', 'tensor', 'fsdp'), may hold values from -0.15625 to 0.15625
- head_bias: bfloat16 [2, 2, 384], P('section', None, ('tensor', 'fsdp')), may hold values from -3 to 3
- up_bias: bfloat16 [2, 1536], P('section', ('tensor', 'fsdp')), may hold values from -3 to 3
- gains: bfloat16 [2, 2, 384], P('section', None, ('tensor', 'fsdp')), may hold values from 0.5 to 1.5
- shifts: bfloat16 [2, 4, 384], P('section', None, ('tensor', 'fsdp')), may hold values from -2 to 2
Outputs:
- activations: bfloat16 [2, 2, 16, 82, 384], P('section', None, ('fsdp', 'tensor'))
- input_grads: bfloat16 [2, 2, 16, 82, 384], P('section', None, ('fsdp', 'tensor'))
- grad_qkv: float32 [2, 384, 3, 384], P('section', 'fsdp', None, 'tensor')
- grad_out: float32 [2, 384, 384], P('section', 'tensor', 'fsdp')
- grad_up: float32 [2, 384, 1536], P('section', 'fsdp', 'tensor')
- grad_down: float32 [2, 1536, 384], P('section', 'tensor', 'fsdp')
- grad_head_bias: float32 [2, 2, 384], P('section', None, ('tensor', 'fsdp'))
- grad_up_bias: float32 [2, 1536], P('section', ('tensor', 'fsdp'))
- grad_gains: float32 [2, 2, 384], P('section', None, ('tensor', 'fsdp'))
- grad_shifts: float32 [2, 4, 384], P('section', None, ('tensor', 'fsdp'))
The draws below stay inside these ranges and needn't reach their ends.
Inputs may be any that keep to these rules, and one draw needn't show every extreme that they name: The first image_count[m, f] image slots of data shard f in micro-batch m hold images, the other slots are empty. In every draw some shard holds 2 images and some holds one.
All inputs are finite; a program needn't handle non-finite values.
Results may differ from the reference program's by a relative error of at most 0.015.
Values may be sent and summed in bfloat16 or wider, within the bound.
No kernel may reach another device: no remote copies, remote signals or barrier semaphores. Data moves between devices by JAX's collectives and lax.ppermute only.
A program may use at most 128 MiB of HBM per device.

```python
import math
import jax
import jax.numpy as jnp
from jax import lax

D = 384
HD = 64
FF = 1536
SEQ = 82
MB = 2
SLOTS = 2
IMAGES = 16
N_FSDP = 8


def draw_image_count(key, part):
    key = jax.random.fold_in(key, 7)
    first_key, full_key, other_key = jax.random.split(key, 3)
    total = MB * N_FSDP
    counts = jax.random.randint(first_key, (total,), 1, SLOTS + 1)
    full = jax.random.randint(full_key, (), 0, total)
    other = (full + jax.random.randint(other_key, (), 1, total)) % total
    places = jnp.arange(total)
    counts = jnp.where(places == full, SLOTS, counts)
    counts = jnp.where(places == other, 1, counts)
    return counts.reshape(MB, N_FSDP).astype(jnp.int32)


def shard_levels(own_key, extent, cuts, low, high):
    level, own = 1.0, jax.random.fold_in(own_key, 6)
    for dim, parts in cuts:
        heights = jnp.exp(jax.random.uniform(jax.random.fold_in(own, dim), (parts,), jnp.float32, low / len(cuts), high / len(cuts)))
        level = level * jnp.repeat(heights, extent[dim] // parts).reshape([-1 if axis == dim else 1 for axis in range(len(extent))])
    return level


def noise(key, shape, deviation, limit, cuts=(), held_as=jnp.bfloat16):
    values = deviation * jax.random.normal(key, shape, jnp.float32)
    if cuts:
        values = values * shard_levels(key, shape, cuts, -0.22, 0.18)
    return jnp.clip(values, -limit, limit).astype(held_as)


def setup_inputs(seed: int = 0) -> dict:
    arg_keys = jax.random.split(jax.random.key(seed), 12)
    return {
        "tokens": noise(arg_keys[0], (MB, IMAGES, SEQ, D), 1.0, 6.0, ((1, 16),)),
        "out_grad": noise(arg_keys[1], (MB, IMAGES, SEQ, D), 1.0, 6.0, ((1, 16),)),
        "image_count": draw_image_count(jax.random.fold_in(arg_keys[11], 71), 0),
        "w_qkv": noise(arg_keys[3], (2, D, 3, D), D ** -0.5, 0.3125, ((0, 2), (1, 8), (3, 2))),
        "w_out": noise(arg_keys[4], (2, D, D), (D // 16) ** -0.5, 1.25, ((0, 2), (1, 2), (2, 8))),
        "w_up": noise(arg_keys[5], (2, D, FF), D ** -0.5, 0.3125, ((0, 2), (1, 8), (2, 2))),
        "w_down": noise(arg_keys[6], (2, FF, D), FF ** -0.5, 0.15625, ((0, 2), (1, 2), (2, 8))),
        "head_bias": noise(arg_keys[7], (2, 2, D), 0.5, 3.0, ((0, 2), (2, 16))),
        "up_bias": noise(arg_keys[8], (2, FF), 0.5, 3.0, ((0, 2), (1, 16))),
        "gains": jnp.clip(1.0 + 0.1 * jax.random.normal(arg_keys[9], (2, 2, D), jnp.float32), 0.5, 1.5).astype(jnp.bfloat16),
        "shifts": noise(arg_keys[10], (2, 4, D), 0.3, 2.0, ((0, 2), (2, 16))),
    }


@jax.custom_vjp
def low(v):
    return lax.optimization_barrier(v.astype(jnp.bfloat16)).astype(jnp.float32)

@jax.custom_vjp
def low_back(v):
    return v

def low_keep(v):
    return (low(v), None)

def low_pass(kept, grad):
    return (grad,)

def back_keep(v):
    return (v, None)

def back_low(kept, grad):
    return (low(grad),)
low.defvjp(low_keep, low_pass)
low_back.defvjp(back_keep, back_low)
EPS = 1e-06
HIGH = lax.Precision.HIGHEST

def normed(value, gain, shift):
    mean = lax.optimization_barrier(jnp.mean(value, axis=-1, keepdims=True))
    centred = value - mean
    var = lax.optimization_barrier(jnp.mean(centred * centred, axis=-1, keepdims=True))
    return centred * lax.rsqrt(var + EPS) * gain + shift

def layer(state, params):
    w_qkv, w_out, w_up, w_down, head_bias, up_bias, gains, shifts = params
    count, seq, width = state.shape
    heads = width // HD
    first = low(normed(state, gains[0], shifts[0]))
    proj = jnp.einsum('gsd,dke->gske', first, w_qkv, precision=HIGH)
    query = low_back(low(proj[:, :, 0] + head_bias[0])).reshape(count, seq, heads, HD)
    keys = low_back(low(proj[:, :, 1])).reshape(count, seq, heads, HD)
    values = low_back(low(proj[:, :, 2] + head_bias[1])).reshape(count, seq, heads, HD)
    scores = low_back(jnp.einsum('gqhe,gkhe->ghqk', query, keys, precision=HIGH) * (1.0 / math.sqrt(HD)))
    probs = low(jax.nn.softmax(scores, axis=-1))
    mixed = jnp.einsum('ghqk,gkhe->gqhe', probs, values, precision=HIGH).reshape(count, seq, width)
    mixed = low_back(low(mixed))
    attn = low_back(jnp.einsum('gsd,de->gse', mixed, w_out, precision=HIGH) + shifts[1])
    resid = state + attn
    second = low(normed(resid, gains[1], shifts[2]))
    hidden = low_back(jnp.einsum('gsd,df->gsf', second, w_up, precision=HIGH) + up_bias)
    active = low(jax.nn.gelu(hidden, approximate=False))
    branch = low_back(jnp.einsum('gsf,fd->gsd', active, w_down, precision=HIGH) + shifts[3])
    return resid + branch

def reference(tokens, out_grad, image_count, w_qkv, w_out, w_up, w_down, head_bias, up_bias, gains, shifts):
    group = math.gcd(IMAGES, 16)
    blocks = IMAGES // group
    slot_ids = jnp.arange(IMAGES, dtype=jnp.int32)
    live = (slot_ids[None, :] % SLOTS < jnp.repeat(image_count, SLOTS, axis=1)).astype(jnp.float32)
    stacked = (w_qkv, w_out, w_up, w_down, head_bias, up_bias, gains, shifts)
    params_a = tuple((p[0].astype(jnp.float32) for p in stacked))
    params_b = tuple((p[1].astype(jnp.float32) for p in stacked))
    zero_a = jax.tree.map(jnp.zeros_like, params_a)
    zero_b = jax.tree.map(jnp.zeros_like, params_b)

    def step(totals, item):
        inputs, cotangent, alive = item
        mask = alive[:, None, None]
        first_in = inputs.astype(jnp.float32)
        out_a, back_a = jax.vjp(layer, first_in, params_a)
        second_in = low(out_a)
        out_b, back_b = jax.vjp(layer, second_in, params_b)
        grad_b_in, grad_b = back_b(cotangent.astype(jnp.float32) * mask)
        grad_b_low = low(grad_b_in)
        grad_a_in, grad_a = back_a(grad_b_low)
        sums_a = jax.tree.map(lambda u, v: u + v, totals[0], grad_a)
        sums_b = jax.tree.map(lambda u, v: u + v, totals[1], grad_b)
        acts_a = (out_a * mask).astype(jnp.bfloat16)
        acts_b = (out_b * mask).astype(jnp.bfloat16)
        return ((sums_a, sums_b), (acts_a, acts_b, grad_a_in.astype(jnp.bfloat16), grad_b_in.astype(jnp.bfloat16)))
    inputs = tokens.reshape(MB * blocks, group, SEQ, D)
    cotangents = out_grad.reshape(MB * blocks, group, SEQ, D)
    alive = live.reshape(MB * blocks, group)
    totals, outs = lax.scan(step, (zero_a, zero_b), (inputs, cotangents, alive))
    acts_a, acts_b, grads_a, grads_b = outs
    shape = (MB, IMAGES, SEQ, D)
    activations = jnp.stack([acts_a.reshape(shape), acts_b.reshape(shape)])
    input_grads = jnp.stack([grads_a.reshape(shape), grads_b.reshape(shape)])
    pairs = [jnp.stack([u, v]) for u, v in zip(totals[0], totals[1])]
    return (activations, input_grads, pairs[0], pairs[1], pairs[2], pairs[3], pairs[4], pairs[5], pairs[6], pairs[7])
```

```python
import functools
import math

import jax
import jax.numpy as jnp
from jax import lax
from jax.experimental import pallas as pl
from jax.experimental.pallas import tpu as pltpu
from jax.sharding import PartitionSpec as P

HD = 64
EPS = 1e-06
INV_ROOT_TWO = 0.7071067811865476
INV_ROOT_TWO_PI = 0.3989422804014327
SCALE = 1.0 / math.sqrt(HD)
BF = jnp.bfloat16
F32 = jnp.float32
GRID_RING = (0, 1, 3, 5, 7, 6, 4, 2)
ROW_STEP = 88
EXT = 128


def dot(a, b, dims):
    return lax.dot_general(a, b, (dims, ((), ())), preferred_element_type=F32)


def nn(a, b):
    return dot(a, b, ((1,), (0,)))


def nt(a, b):
    return dot(a, b, ((1,), (1,)))


def tn(a, b):
    return dot(a, b, ((0,), (0,)))


def norm(value):
    mean = jnp.mean(value, axis=-1, keepdims=True)
    centred = value - mean
    var = jnp.mean(centred * centred, axis=-1, keepdims=True)
    factor = lax.rsqrt(var + EPS)
    return centred * factor, factor


def norm_back(grad, unit, factor, gain):
    scaled = grad * gain
    plain = jnp.mean(scaled, axis=-1, keepdims=True)
    along = jnp.mean(scaled * unit, axis=-1, keepdims=True)
    return (scaled - plain - unit * along) * factor


class Dims:
    def __init__(self, seq, width, hidden, shards):
        self.seq, self.width, self.hidden, self.shards = seq, width, hidden, shards
        self.half = width // 2
        self.fh = hidden // 2
        self.heads = self.half // HD
        self.o_out = 3 * self.half
        self.o_up = self.o_out + self.half
        self.o_down = self.o_up + self.fh
        self.cols = self.o_down + self.fh
        self.packed = self.cols + EXT
        self.rows = 2 * ROW_STEP
        self.groups = width // 128

    def state_shapes(self):
        r, w = self.rows, self.width
        return dict(
            unit_one=((r, w), F32),
            factors=((2, r, 1), F32),
            first=((r, w), BF),
            proj=((2, r, 3 * self.half), F32),
            probs=((4 * self.heads, ROW_STEP, ROW_STEP), F32),
            mixed=((2, r, self.half), F32),
            unit_two=((r, w), F32),
            second=((r, w), BF),
            slope=((2, r, self.fh), F32),
            active=((2, r, self.fh), BF),
        )


def layer_forward(dm, state, w, vecs, st):
    half, fh = dm.half, dm.fh
    unit, factor = norm(state)
    st["unit_one"][...] = unit
    st["factors"][0] = factor
    first = (unit * vecs[0:1, :] + vecs[2:3, :]).astype(BF)
    st["first"][...] = first
    attn = None
    for t in range(2):
        proj = nn(first, w[t, :, 0 : 3 * half])
        query = proj[:, 0:half] + vecs[6:7, t * half : (t + 1) * half]
        keys = proj[:, half : 2 * half]
        values = proj[:, 2 * half :] + vecs[7:8, t * half : (t + 1) * half]
        st["proj"][t, :, 0:half] = query
        st["proj"][t, :, half : 2 * half] = keys
        st["proj"][t, :, 2 * half :] = values
        column = lax.broadcasted_iota(jnp.int32, (ROW_STEP, ROW_STEP), 1)
        for m in range(2):
            rows = slice(m * ROW_STEP, (m + 1) * ROW_STEP)
            for h in range(dm.heads):
                cols = slice(h * HD, (h + 1) * HD)
                scores = nt(query[rows, cols].astype(BF), keys[rows, cols].astype(BF)) * SCALE
                scores = jnp.where(column < dm.seq, scores, -1e30)
                top = jnp.max(scores, axis=-1, keepdims=True)
                expo = jnp.exp(scores - top)
                probs = expo / jnp.sum(expo, axis=-1, keepdims=True)
                st["probs"][(t * 2 + m) * dm.heads + h] = probs
                st["mixed"][t, rows, cols] = nn(probs.astype(BF), values[rows, cols].astype(BF))
        part = nt(st["mixed"][t].astype(BF), w[t, :, dm.o_out : dm.o_out + half])
        attn = part if attn is None else attn + part
    resid = state + attn + vecs[3:4, :]
    unit, factor = norm(resid)
    st["unit_two"][...] = unit
    st["factors"][1] = factor
    second = (unit * vecs[1:2, :] + vecs[4:5, :]).astype(BF)
    st["second"][...] = second
    output = resid + vecs[5:6, :]
    per = fh // dm.width
    for t in range(2):
        bias = jnp.concatenate([vecs[8 + t * per + j : 9 + t * per + j, :] for j in range(per)], axis=1)
        hidden = nn(second, w[t, :, dm.o_up : dm.o_up + fh]) + bias
        curve = 0.5 * (1.0 + lax.erf(hidden * INV_ROOT_TWO))
        st["slope"][t] = curve + hidden * jnp.exp(-0.5 * hidden * hidden) * INV_ROOT_TWO_PI
        active = (hidden * curve).astype(BF)
        st["active"][t] = active
        output += nt(active, w[t, :, dm.o_down : dm.o_down + fh])
    return output


def total_rows(value):
    return jnp.sum(value, axis=0, keepdims=True)


def layer_backward(dm, grad, w, vecs, st, grads, gproj, tensor):
    half, fh = dm.half, dm.fh
    low = grad.astype(BF)
    shift_branch = total_rows(low.astype(F32))
    second = st["second"][...]
    up_bias = []
    grad_second = None
    for t in range(2):
        grads[t][:, dm.o_down : dm.o_down + fh] = tn(low, st["active"][t]).astype(BF)
        raw = nn(low, w[t, :, dm.o_down : dm.o_down + fh]) * st["slope"][t]
        up_bias.append(total_rows(raw))
        grad_hidden = raw.astype(BF)
        grads[t][:, dm.o_up : dm.o_up + fh] = tn(second, grad_hidden).astype(BF)
        part = nt(grad_hidden, w[t, :, dm.o_up : dm.o_up + fh])
        grad_second = part if grad_second is None else grad_second + part
    unit = st["unit_two"][...]
    gain_two, shift_two = total_rows(grad_second * unit), total_rows(grad_second)
    grad_resid = grad + norm_back(grad_second, unit, st["factors"][1], vecs[1:2, :])
    low = grad_resid.astype(BF)
    shift_attn = total_rows(low.astype(F32))
    first = st["first"][...]
    bias_query, bias_values = [], []
    grad_first = None
    for t in range(2):
        grads[t][:, dm.o_out : dm.o_out + half] = tn(low, st["mixed"][t].astype(BF)).astype(BF)
        grad_mixed = nn(low, w[t, :, dm.o_out : dm.o_out + half])
        for m in range(2):
            rows = slice(m * ROW_STEP, (m + 1) * ROW_STEP)
            for h in range(dm.heads):
                cols = slice(h * HD, (h + 1) * HD)
                query = st["proj"][t, rows, h * HD : (h + 1) * HD].astype(BF)
                keys = st["proj"][t, rows, half + h * HD : half + (h + 1) * HD].astype(BF)
                values = st["proj"][t, rows, 2 * half + h * HD : 2 * half + (h + 1) * HD].astype(BF)
                probs = st["probs"][(t * 2 + m) * dm.heads + h]
                gm = grad_mixed[rows, cols].astype(BF)
                gproj[rows, 2 * half + h * HD : 2 * half + (h + 1) * HD] = tn(probs.astype(BF), gm)
                gp = nt(gm, values)
                inner = jnp.sum(gp * probs, axis=-1, keepdims=True)
                gs = (probs * (gp - inner)).astype(BF)
                gproj[rows, h * HD : (h + 1) * HD] = nn(gs, keys) * SCALE
                gproj[rows, half + h * HD : half + (h + 1) * HD] = tn(gs, query) * SCALE
        bias_query.append(total_rows(gproj[:, 0:half]))
        bias_values.append(total_rows(gproj[:, 2 * half :]))
        grad_proj = gproj[...].astype(BF)
        grads[t][:, 0 : 3 * half] = tn(first, grad_proj).astype(BF)
        part = nt(grad_proj, w[t, :, 0 : 3 * half])
        grad_first = part if grad_first is None else grad_first + part
    unit = st["unit_one"][...]
    gain_one, shift_one = total_rows(grad_first * unit), total_rows(grad_first)
    grad_state = grad_resid + norm_back(grad_first, unit, st["factors"][0], vecs[0:1, :])
    own_first = tensor == 0

    def by_half(vec):
        low_half, high_half = vec[:, 0:half], vec[:, half:]
        return jnp.where(own_first, low_half, high_half), jnp.where(own_first, high_half, low_half)

    plain = [by_half(v) for v in (gain_one, gain_two, shift_one, shift_attn, shift_two, shift_branch)]
    share, up_share = half // dm.shards, fh // dm.shards
    block = dm.width // dm.shards
    for t in range(2):
        rows = [v[t] for v in plain] + [bias_query[t], bias_values[t]]
        stack = jnp.concatenate(rows, axis=0)
        for f in range(dm.shards):
            grads[t][f * block : (f + 1) * block, dm.cols :] = jnp.zeros((block, EXT), BF)
            piece = jnp.concatenate([stack[:, f * share : (f + 1) * share], jnp.zeros((8, EXT - share), F32)], axis=1)
            up_piece = up_bias[t][:, f * up_share : (f + 1) * up_share]
            up_piece = jnp.concatenate([up_piece, jnp.zeros((1, EXT - up_share), F32)], axis=1)
            piece = jnp.concatenate([piece, up_piece, jnp.zeros((7, EXT), F32)], axis=0)
            grads[t][f * block : f * block + 16, dm.cols :] = piece.astype(BF)
    return grad_state


def spread(dm, ref, get):
    pad = jnp.zeros((ROW_STEP - dm.seq, dm.width), F32)
    for m in range(2):
        ref[m * ROW_STEP : m * ROW_STEP + dm.seq, :] = get(m)
        ref[m * ROW_STEP + dm.seq : (m + 1) * ROW_STEP, :] = pad


def image(dm, value, m):
    return value[m * ROW_STEP : m * ROW_STEP + dm.seq, :]


def kernel_first(dm, count, order, tokens, *refs):
    pieces, refs = refs[: 2 * count], refs[2 * count :]
    w, vecs, out = refs[0:3]
    names = list(dm.state_shapes())
    st = dict(zip(names, refs[3 : 3 + len(names)]))
    rows = refs[3 + len(names)]
    block = dm.width // dm.shards
    ext = jnp.zeros((block, EXT), F32)
    for t in range(2):
        for i in range(count):
            ref = pieces[t * count + i]
            place = pl.ds(pl.multiple_of(order[i] * block, 16), block)
            w[t, place, :] = ref[:, 0 : dm.cols]
            ext += ref[:, dm.cols :].astype(F32)
    g = dm.groups
    for v in range(6):
        vecs[v : v + 1, :] = jnp.concatenate([ext[v * g + j : v * g + j + 1, :] for j in range(g)], axis=1)
    own_first = lax.axis_index("tensor") == 0
    for v in (6, 7):
        row = jnp.concatenate([ext[v * g + j : v * g + j + 1, :] for j in range(g)], axis=1)
        turned = jnp.concatenate([row[:, dm.half :], row[:, 0 : dm.half]], axis=1)
        vecs[v : v + 1, :] = jnp.where(own_first, row, turned)
    per = dm.hidden // dm.width
    up = [
        jnp.concatenate([ext[(8 + v) * g + j : (8 + v) * g + j + 1, :] for j in range(g)], axis=1)
        for v in range(per)
    ]
    for v in range(per):
        vecs[8 + v : 9 + v, :] = jnp.where(own_first, up[v], up[(v + per // 2) % per])
    spread(dm, rows, lambda m: tokens[m, 0].astype(F32))
    output = layer_forward(dm, rows[...], w, vecs, st)
    for m in range(2):
        out[m, 0] = image(dm, output, m).astype(BF)


def live_of(count_ref, m):
    return (lax.axis_index("tensor") < count_ref[m, 0]).astype(F32)


def kernel_second(dm, count_ref, h0, h1, out_grad, w, vecs, acts, grad_in, grad_own, grad_other, *scratch):
    names = list(dm.state_shapes())
    st = dict(zip(names, scratch[: len(names)]))
    rows, gproj = scratch[len(names) :]
    section = lax.axis_index("section")

    @pl.when(section == 0)
    def _():
        for m in range(2):
            acts[m, 0] = (h0[m, 0].astype(F32) * live_of(count_ref, m)).astype(BF)

    @pl.when(section != 0)
    def _():
        spread(dm, rows, lambda m: h1[m, 0].astype(F32))
        output = layer_forward(dm, rows[...], w, vecs, st)
        for m in range(2):
            acts[m, 0] = (image(dm, output, m) * live_of(count_ref, m)).astype(BF)
        spread(dm, rows, lambda m: out_grad[m, 0].astype(F32) * live_of(count_ref, m))
        grad = layer_backward(
            dm, rows[...], w, vecs, st, (grad_own, grad_other), gproj, lax.axis_index("tensor")
        )
        for m in range(2):
            grad_in[m, 0] = image(dm, grad, m).astype(BF)


def kernel_third(dm, incoming, w, vecs, own, given_own, given_other, *refs):
    names = list(dm.state_shapes())
    st = dict(zip(names, refs[: len(names)]))
    grad_in, grad_own, grad_other, rows, gproj = refs[len(names) :]

    @pl.when(lax.axis_index("section") == 0)
    def _():
        spread(dm, rows, lambda m: incoming[m, 0].astype(F32))
        grad = layer_backward(
            dm, rows[...], w, vecs, st, (grad_own, grad_other), gproj, lax.axis_index("tensor")
        )
        for m in range(2):
            grad_in[m, 0] = image(dm, grad, m).astype(BF)

    @pl.when(lax.axis_index("section") != 0)
    def _():
        grad_in[...] = own[...]
        grad_own[...] = given_own[...]
        grad_other[...] = given_other[...]


def kernel_pack(dm, w_qkv, w_out, w_up, w_down, head_bias, up_bias, gains, shifts, packed):
    half, fh = dm.half, dm.fh
    block = dm.width // dm.shards
    for k in range(3):
        packed[:, k * half : (k + 1) * half] = w_qkv[0, :, k, :]
    row = lax.broadcasted_iota(jnp.int32, (block, block), 0)
    column = lax.broadcasted_iota(jnp.int32, (block, block), 1)
    eye = (row == column).astype(BF)
    packed[:, dm.o_out : dm.o_out + half] = nt(eye, w_out[0]).astype(BF)
    packed[:, dm.o_up : dm.o_up + fh] = w_up[0]
    packed[:, dm.o_down : dm.o_down + fh] = nt(eye, w_down[0]).astype(BF)
    place = lax.axis_index("tensor") * dm.shards + lax.axis_index("fsdp")

    def placed(values, total):
        share = values.shape[1]
        row = lax.broadcasted_iota(jnp.int32, (share, total), 0)
        column = lax.broadcasted_iota(jnp.int32, (share, total), 1)
        return nn(values, (column == row + place * share).astype(BF))

    small = jnp.concatenate([gains[0], shifts[0], head_bias[0]], axis=0)
    small = placed(small, dm.width)
    up = placed(up_bias[...], dm.hidden)
    rows = []
    for v in range(8):
        rows += [small[v : v + 1, j * 128 : (j + 1) * 128] for j in range(dm.groups)]
    rows += [up[:, j * 128 : (j + 1) * 128] for j in range(dm.hidden // 128)]
    rows.append(jnp.zeros((block - len(rows), EXT), F32))
    packed[:, dm.cols :] = jnp.concatenate(rows, axis=0).astype(BF)


def kernel_unpack(dm, mine, left, right, g_qkv, g_out, g_up, g_down, g_head, g_upb, g_gain, g_shift, scratch):
    half, fh = dm.half, dm.fh
    block = dm.width // dm.shards
    value = mine[...].astype(F32) + left[...].astype(F32) + right[...].astype(F32)
    for k in range(3):
        g_qkv[0, :, k, :] = value[:, k * half : (k + 1) * half]
    g_up[0] = value[:, dm.o_up : dm.o_up + fh]
    scratch[...] = jnp.zeros_like(scratch)
    scratch[0:block, 0:half] = value[:, dm.o_out : dm.o_out + half]
    scratch[0:block, 2 * 128 : 2 * 128 + fh] = value[:, dm.o_down : dm.o_down + fh]
    turned = scratch[...].T
    g_out[0] = turned[0:half, 0:block]
    g_down[0] = turned[256 : 256 + fh, 0:block]
    ext = value[0:16, dm.cols :]
    share, up_share = half // dm.shards, fh // dm.shards
    g_gain[0] = ext[0:2, 0:share]
    g_shift[0] = ext[2:6, 0:share]
    g_head[0] = ext[6:8, 0:share]
    g_upb[...] = ext[8:9, 0:up_share]


VM = pl.BlockSpec(memory_space=pltpu.VMEM)
SM = pl.BlockSpec(memory_space=pltpu.SMEM)


def call(kernel, ins, outs, args, scratch=(), limit=48):
    return pl.pallas_call(
        kernel,
        in_specs=ins,
        out_specs=[VM] * len(outs),
        out_shape=[jax.ShapeDtypeStruct(s, d) for s, d in outs],
        scratch_shapes=list(scratch),
        compiler_params=pltpu.CompilerParams(vmem_limit_bytes=limit * 2**20),
    )(*args)


def shifted(value, cycle, step):
    count = len(cycle)
    return lax.ppermute(value, "fsdp", [(cycle[i], cycle[(i + step) % count]) for i in range(count)])


def gather_ring(block, cycle):
    count = len(cycle)
    ahead = behind = block
    found = [block]
    offsets = [0]
    for step in range(1, count // 2 + 1):
        if step < count - step:
            ahead, behind = shifted(ahead, cycle, 1), shifted(behind, cycle, -1)
            found += [ahead, behind]
            offsets += [-step, step]
        else:
            cut = block.shape[1] // 256 * 128
            low, high = shifted(ahead[:, :cut], cycle, 1), shifted(behind[:, cut:], cycle, -1)
            found.append(jnp.concatenate([low, high], axis=1))
            offsets.append(step)
    return found, offsets


def reduce_ring(parts, place, cycle):
    count = len(cycle)
    table = jnp.array(cycle, jnp.int32)
    cut = parts.shape[2] // 256 * 128

    def part(offset, lo, hi):
        dest = table[lax.rem(place + offset + count, count)]
        return lax.dynamic_index_in_dim(parts, dest, 0, keepdims=False)[:, lo:hi]

    def add(a, b):
        return (a.astype(F32) + b.astype(F32)).astype(BF)

    far = count // 2
    low = shifted(part(far, 0, cut), cycle, 1)
    high = shifted(part(-far, cut, None), cycle, -1)
    for step in range(far - 1, 0, -1):
        ahead, behind = part(step, 0, None), part(-step, 0, None)
        if step == far - 1:
            ahead = jnp.concatenate([add(ahead[:, :cut], low), ahead[:, cut:]], axis=1)
            behind = jnp.concatenate([behind[:, :cut], add(behind[:, cut:], high)], axis=1)
        else:
            ahead, behind = add(ahead, left), add(behind, right)
        left, right = shifted(ahead, cycle, 1), shifted(behind, cycle, -1)
    return part(0, 0, None), left, right


def per_device(tokens, out_grad, image_count, w_qkv, w_out, w_up, w_down, head_bias, up_bias, gains, shifts):
    seq, width = tokens.shape[2:]
    shards = lax.axis_size("fsdp")
    ring = shards == len(GRID_RING)
    hidden = w_up.shape[2] * 2
    dm = Dims(seq, width, hidden, len(GRID_RING))
    block = width // dm.shards
    swap = [(0, 1), (1, 0)]
    vectors = (head_bias, up_bias, gains, shifts)
    if ring:
        packed = call(
            functools.partial(kernel_pack, dm),
            [VM] * 8,
            [((block, dm.packed), BF)],
            (w_qkv, w_out, w_up, w_down) + vectors,
        )[0]
        found, offsets = gather_ring(packed, GRID_RING)
        table = jnp.array(GRID_RING, jnp.int32)
        inverse = [GRID_RING.index(i) for i in range(len(GRID_RING))]
        place = jnp.array(inverse, jnp.int32)[lax.axis_index("fsdp")]
        order = table[lax.rem(place + jnp.array(offsets, jnp.int32) + dm.shards, dm.shards)]
    else:
        rows = jnp.concatenate(
            [
                w_qkv[0].reshape(w_qkv.shape[1], -1),
                w_out[0].T,
                w_up[0],
                w_down[0].T,
            ],
            axis=1,
        )
        rows = lax.all_gather(rows, "fsdp", axis=0, tiled=True)
        whole = [
            lax.all_gather(v[0], ("tensor", "fsdp"), axis=v.ndim - 2, tiled=True).reshape(-1, 128)
            for v in (gains, shifts, head_bias, up_bias)
        ]
        ext = jnp.concatenate(whole, axis=0)
        ext = jnp.pad(ext, ((0, block - ext.shape[0]), (0, 0)))
        ext = jnp.where(lax.axis_index("tensor") == 0, ext, jnp.zeros_like(ext))
        ext = jnp.pad(ext, ((0, width - block), (0, 0)))
        rows = jnp.concatenate([rows, ext], axis=1)
        found = [rows[i * block : (i + 1) * block] for i in range(dm.shards)]
        order = jnp.arange(dm.shards, dtype=jnp.int32)
    others = [lax.ppermute(b, "tensor", swap) for b in found]
    states = list(dm.state_shapes().values())
    shape = tokens.shape
    scratch_rows = pltpu.VMEM((dm.rows, width), F32)
    scratch_proj = pltpu.VMEM((dm.rows, 3 * dm.half), F32)
    w, vecs, low0, *state = call(
        functools.partial(kernel_first, dm, len(found)),
        [SM] + [VM] * (1 + 2 * len(found)),
        [((2, width, dm.cols), BF), ((16, width), F32), (shape, BF)] + states,
        (order, tokens) + tuple(found) + tuple(others),
        scratch=[scratch_rows],
    )
    h1 = lax.ppermute(low0, "section", [(0, 1)])
    packed_grads = [((width, dm.packed), BF)] * 2
    acts, grad1, own, other = call(
        functools.partial(kernel_second, dm),
        [SM] + [VM] * 5,
        [(shape, BF), (shape, BF)] + packed_grads,
        (image_count, low0, h1, out_grad, w, vecs),
        scratch=[pltpu.VMEM(s, d) for s, d in states] + [scratch_rows, scratch_proj],
    )
    incoming = lax.ppermute(grad1, "section", [(1, 0)])
    in_grads, own, other = call(
        functools.partial(kernel_third, dm),
        [VM] * (6 + len(states)),
        [(shape, BF)] + packed_grads,
        (incoming, w, vecs, grad1, own, other) + tuple(state),
        scratch=[scratch_rows, scratch_proj],
    )
    mine = own.astype(F32) + lax.ppermute(other, "tensor", swap).astype(F32)
    if ring:
        parts = mine.astype(BF).reshape(dm.shards, block, dm.packed)
        terms = reduce_ring(parts, place, GRID_RING)
        grads = call(
            functools.partial(kernel_unpack, dm),
            [VM] * 3,
            [(v.shape, F32) for v in (w_qkv, w_out, w_up, w_down) + vectors],
            terms,
            scratch=[pltpu.VMEM((128, 256 + dm.fh), F32)],
        )
    else:
        half = dm.half
        body = lax.psum_scatter(mine[:, : dm.cols], "fsdp", scatter_dimension=0, tiled=True)
        share, up_share = half // dm.shards, dm.fh // dm.shards
        ext = mine[:, dm.cols :].reshape(dm.shards, block, EXT)
        small = jnp.moveaxis(ext[:, 0:8, 0:share], 0, 1).reshape(8, half)
        small = lax.psum_scatter(small, "fsdp", scatter_dimension=1, tiled=True)
        up = lax.psum_scatter(ext[:, 8, 0:up_share].reshape(-1), "fsdp", scatter_dimension=0, tiled=True)
        grads = [
            body[:, : 3 * half].reshape(w_qkv.shape),
            body[:, dm.o_out : dm.o_up].T[None],
            body[:, dm.o_up : dm.o_down][None],
            body[:, dm.o_down :].T[None],
            small[6:8][None],
            up[None],
            small[0:2][None],
            small[2:6][None],
        ]
    return (acts[None], in_grads[None], *grads)


def solution(mesh):
    both = ("tensor", "fsdp")
    params = (
        P("section", "fsdp", None, "tensor"),
        P("section", "tensor", "fsdp"),
        P("section", "fsdp", "tensor"),
        P("section", "tensor", "fsdp"),
        P("section", None, both),
        P("section", both),
        P("section", None, both),
        P("section", None, both),
    )
    images = P(None, ("fsdp", "tensor"), None, None)
    layered = P("section", None, ("fsdp", "tensor"), None, None)
    return jax.shard_map(
        per_device,
        mesh=mesh,
        in_specs=(images, images, P(None, "fsdp")) + params,
        out_specs=(layered, layered) + params,
        check_vma=False,
    )
```

```python
import functools
import math

import jax
import jax.numpy as jnp
from jax import lax
from jax.experimental import pallas as pl
from jax.experimental.pallas import tpu as pltpu
from jax.sharding import PartitionSpec as P

HD = 64
EPS = 1e-06
INV_ROOT_TWO = 0.7071067811865476
INV_ROOT_TWO_PI = 0.3989422804014327
SCALE = 1.0 / math.sqrt(HD)
BF = jnp.bfloat16
F32 = jnp.float32
GRID_RING = (0, 1, 3, 5, 7, 6, 4, 2)
RING_PLACE = tuple(GRID_RING.index(i) for i in range(len(GRID_RING)))
NEAR = 2
ROW_STEP = 88
EXT = 128


def dot(a, b, dims):
    return lax.dot_general(a, b, (dims, ((), ())), preferred_element_type=F32)


def nn(a, b):
    return dot(a, b, ((1,), (0,)))


def nt(a, b):
    return dot(a, b, ((1,), (1,)))


def tn(a, b):
    return dot(a, b, ((0,), (0,)))


def norm(value):
    mean = jnp.mean(value, axis=-1, keepdims=True)
    centred = value - mean
    var = jnp.mean(centred * centred, axis=-1, keepdims=True)
    factor = lax.rsqrt(var + EPS)
    return centred * factor, factor


def norm_back(grad, unit, factor, gain):
    scaled = grad * gain
    plain = jnp.mean(scaled, axis=-1, keepdims=True)
    along = jnp.mean(scaled * unit, axis=-1, keepdims=True)
    return (scaled - plain - unit * along) * factor


def picked(options, index):
    value = jnp.int32(options[0])
    for i in range(1, len(options)):
        value = jnp.where(index == i, jnp.int32(options[i]), value)
    return value


class Dims:
    def __init__(self, seq, width, hidden, shards):
        self.seq, self.width, self.hidden, self.shards = seq, width, hidden, shards
        self.half = width // 2
        self.fh = hidden // 2
        self.heads = self.half // HD
        self.o_out = 3 * self.half
        self.o_up = self.o_out + self.half
        self.o_down = self.o_up + self.fh
        self.cols = self.o_down + self.fh
        self.packed = self.cols + EXT
        self.rows = 2 * ROW_STEP
        self.groups = width // 128

    def state_shapes(self):
        r, w = self.rows, self.width
        return dict(
            proj=((2, r, 3 * self.half), F32),
            probs=((4 * self.heads, ROW_STEP, ROW_STEP), F32),
            mixed=((2, r, self.half), F32),
            unit_one=((r, w), F32),
            factors=((2, r, 1), F32),
            first=((r, w), BF),
            unit_two=((r, w), F32),
            second=((r, w), BF),
            slope=((2, r, self.fh), F32),
            active=((2, r, self.fh), BF),
        )

    def cotangent_shapes(self):
        r, w = self.rows, self.width
        return dict(
            branch=((r, w), BF),
            hidden=((2, r, self.fh), BF),
            attn=((r, w), BF),
            proj=((2, r, 3 * self.half), F32),
            vecs=((16, w), F32),
        )

    def work_shapes(self):
        return dict(
            rows=((self.rows, self.width), F32),
            mixed=((2, self.rows, self.half), F32),
            scores=((4 * self.heads, ROW_STEP, ROW_STEP), F32),
        )

    def cells(self):
        for t in range(2):
            for m in range(2):
                for h in range(self.heads):
                    rows = slice(m * ROW_STEP, (m + 1) * ROW_STEP)
                    yield (t * 2 + m) * self.heads + h, t, rows, h * HD


def layer_forward(dm, state, w, vecs, st, keep, weights_ready=None):
    half, fh = dm.half, dm.fh
    unit, factor = norm(state)
    first = (unit * vecs[0:1, :] + vecs[2:3, :]).astype(BF)
    if keep:
        st["unit_one"][...] = unit
        st["factors"][0] = factor
        st["first"][...] = first
    proj, mixed = st["proj"], st["mixed"]
    for t in range(2):
        value = nn(first, w[t, :, 0 : 3 * half])
        proj[t, :, 0:half] = value[:, 0:half] + vecs[6:7, t * half : (t + 1) * half]
        proj[t, :, half : 2 * half] = value[:, half : 2 * half]
        proj[t, :, 2 * half :] = value[:, 2 * half :] + vecs[7:8, t * half : (t + 1) * half]
    for i, t, rows, c in dm.cells():
        query, keys = proj[t, rows, c : c + HD], proj[t, rows, half + c : half + c + HD]
        st["probs"][i] = nt(query.astype(BF), keys.astype(BF))
    scores = st["probs"][...] * SCALE
    column = lax.broadcasted_iota(jnp.int32, scores.shape, 2)
    scores = jnp.where(column < dm.seq, scores, -1e30)
    expo = jnp.exp(scores - jnp.max(scores, axis=-1, keepdims=True))
    st["probs"][...] = expo * (1.0 / jnp.sum(expo, axis=-1, keepdims=True))
    for i, t, rows, c in dm.cells():
        values = proj[t, rows, 2 * half + c : 2 * half + c + HD]
        mixed[t, rows, c : c + HD] = nn(st["probs"][i].astype(BF), values.astype(BF))
    resid = state + vecs[3:4, :]
    for t in range(2):
        resid += nt(mixed[t].astype(BF), w[t, :, dm.o_out : dm.o_out + half])
    unit, factor = norm(resid)
    second = (unit * vecs[1:2, :] + vecs[4:5, :]).astype(BF)
    if keep:
        st["unit_two"][...] = unit
        st["factors"][1] = factor
        st["second"][...] = second
    output = resid + vecs[5:6, :]
    per = fh // dm.width
    if weights_ready is not None:
        weights_ready()
    for t in range(2):
        bias = jnp.concatenate([vecs[8 + t * per + j : 9 + t * per + j, :] for j in range(per)], axis=1)
        hidden = nn(second, w[t, :, dm.o_up : dm.o_up + fh]) + bias
        curve = 0.5 * (1.0 + lax.erf(hidden * INV_ROOT_TWO))
        active = (hidden * curve).astype(BF)
        if keep:
            st["slope"][t] = curve + hidden * jnp.exp(-0.5 * hidden * hidden) * INV_ROOT_TWO_PI
            st["active"][t] = active
        output += nt(active, w[t, :, dm.o_down : dm.o_down + fh])
    return output


def total_rows(value):
    return jnp.sum(value, axis=0, keepdims=True)


def layer_backward(dm, grad, w, vecs, st, ct, work):
    half, fh = dm.half, dm.fh
    low = grad.astype(BF)
    ct["branch"][...] = low
    shift_branch = total_rows(low.astype(F32))
    per = fh // dm.width
    grad_second = None
    for t in range(2):
        raw = nn(low, w[t, :, dm.o_down : dm.o_down + fh]) * st["slope"][t]
        up_bias = total_rows(raw)
        for j in range(per):
            ct["vecs"][8 + t * per + j : 9 + t * per + j, :] = up_bias[:, j * dm.width : (j + 1) * dm.width]
        grad_hidden = raw.astype(BF)
        ct["hidden"][t] = grad_hidden
        part = nt(grad_hidden, w[t, :, dm.o_up : dm.o_up + fh])
        grad_second = part if grad_second is None else grad_second + part
    unit = st["unit_two"][...]
    gain_two, shift_two = total_rows(grad_second * unit), total_rows(grad_second)
    grad_resid = grad + norm_back(grad_second, unit, st["factors"][1], vecs[1:2, :])
    low = grad_resid.astype(BF)
    ct["attn"][...] = low
    shift_attn = total_rows(low.astype(F32))
    proj, gproj, gmix, scores = st["proj"], ct["proj"], work["mixed"], work["scores"]
    for t in range(2):
        gmix[t] = nn(low, w[t, :, dm.o_out : dm.o_out + half])
    for i, t, rows, c in dm.cells():
        values = proj[t, rows, 2 * half + c : 2 * half + c + HD].astype(BF)
        gm = gmix[t, rows, c : c + HD].astype(BF)
        scores[i] = nt(gm, values)
        gproj[t, rows, 2 * half + c : 2 * half + c + HD] = tn(st["probs"][i].astype(BF), gm)
    probs, gp = st["probs"][...], scores[...]
    scores[...] = probs * (gp - jnp.sum(gp * probs, axis=-1, keepdims=True)) * SCALE
    for i, t, rows, c in dm.cells():
        query = proj[t, rows, c : c + HD].astype(BF)
        keys = proj[t, rows, half + c : half + c + HD].astype(BF)
        gs = scores[i].astype(BF)
        gproj[t, rows, c : c + HD] = nn(gs, keys)
        gproj[t, rows, half + c : half + c + HD] = tn(gs, query)
    grad_first = None
    for t in range(2):
        ct["vecs"][6:7, t * half : (t + 1) * half] = total_rows(gproj[t, :, 0:half])
        ct["vecs"][7:8, t * half : (t + 1) * half] = total_rows(gproj[t, :, 2 * half :])
        part = nt(gproj[t].astype(BF), w[t, :, 0 : 3 * half])
        grad_first = part if grad_first is None else grad_first + part
    unit = st["unit_one"][...]
    gain_one, shift_one = total_rows(grad_first * unit), total_rows(grad_first)
    for i, v in enumerate((gain_one, gain_two, shift_one, shift_attn, shift_two, shift_branch)):
        ct["vecs"][i : i + 1, :] = v
    return grad_resid + norm_back(grad_first, unit, st["factors"][0], vecs[0:1, :])


def parameter_grads(dm, st, ct, grads, slots):
    half, fh = dm.half, dm.fh
    block = dm.width // dm.shards

    def keep(t, column, value):
        for f in range(dm.shards):
            rows = value[f * block : (f + 1) * block].astype(BF)
            grads[t][slots[f], :, column : column + value.shape[1]] = rows

    for t in range(2):
        keep(t, dm.o_down, tn(ct["branch"][...], st["active"][t]))
        keep(t, dm.o_up, tn(st["second"][...], ct["hidden"][t]))
        keep(t, dm.o_out, tn(ct["attn"][...], st["mixed"][t].astype(BF)))
        keep(t, 0, tn(st["first"][...], ct["proj"][t].astype(BF)))
    own_first = lax.axis_index("tensor") == 0
    plain = ct["vecs"][0:6, :]
    turned = jnp.concatenate([plain[:, half:], plain[:, 0:half]], axis=1)
    plain = jnp.where(own_first, plain, turned)
    share, up_share = half // dm.shards, fh // dm.shards
    per = fh // dm.width
    for t in range(2):
        stack = jnp.concatenate([plain, ct["vecs"][6:8, :]], axis=0)[:, t * half : (t + 1) * half]
        up = jnp.concatenate([ct["vecs"][8 + t * per + j : 9 + t * per + j, :] for j in range(per)], axis=1)
        for f in range(dm.shards):
            piece = jnp.concatenate([stack[:, f * share : (f + 1) * share], jnp.zeros((8, EXT - share), F32)], axis=1)
            up_piece = up[:, f * up_share : (f + 1) * up_share]
            up_piece = jnp.concatenate([up_piece, jnp.zeros((1, EXT - up_share), F32)], axis=1)
            piece = jnp.concatenate([piece, up_piece, jnp.zeros((block - 9, EXT), F32)], axis=0)
            grads[t][slots[f], :, dm.cols :] = piece.astype(BF)


def spread(dm, ref, get):
    pad = jnp.zeros((ROW_STEP - dm.seq, dm.width), F32)
    for m in range(2):
        ref[m * ROW_STEP : m * ROW_STEP + dm.seq, :] = get(m)
        ref[m * ROW_STEP + dm.seq : (m + 1) * ROW_STEP, :] = pad


def image(dm, value, m):
    return value[m * ROW_STEP : m * ROW_STEP + dm.seq, :]


def named(shapes, refs):
    return dict(zip(shapes, refs)), refs[len(shapes) :]


def kernel_first(dm, layout, ring, tokens, *refs):
    count = len(layout)
    pieces, refs = refs[: 2 * count], refs[2 * count :]
    w, vecs, out, proj, probs, mixed, rows, extra, sems = refs
    st = dict(proj=proj, probs=probs, mixed=mixed)
    block = dm.width // dm.shards
    early, late = [], []
    if ring:
        place = picked(RING_PLACE, lax.axis_index("fsdp"))
    for t in range(2):
        for i, (offset, start) in enumerate(layout):
            piece = pieces[t * count + i]
            if ring:
                owner = picked([GRID_RING[(p + offset) % dm.shards] for p in range(dm.shards)], place)
                where = pl.ds(pl.multiple_of(owner * block, 16), block)
            else:
                owner = offset
                where = pl.ds(offset * block, block)
            stop = start + piece.shape[1]
            bounds = (0, dm.o_up, dm.cols, dm.packed)
            for j in range(3):
                lo, hi = max(start, bounds[j]), min(stop, bounds[j + 1])
                if lo < hi:
                    target = extra.at[t, owner] if j == 2 else w.at[t, where, pl.ds(lo, hi - lo)]
                    copy = pltpu.make_async_copy(
                        piece.at[:, pl.ds(lo - start, hi - lo)], target, sems.at[j, t * count + i]
                    )
                    (late if j == 1 else early).append(copy)
    for copy in early + late:
        copy.start()
    spread(dm, rows, lambda m: tokens[m, 0].astype(F32))
    for copy in early:
        copy.wait()
    share, up_share = dm.half // dm.shards, dm.fh // dm.shards
    small = [
        jnp.concatenate([extra[t, f].astype(F32)[0:8, 0:share] for f in range(dm.shards)], axis=1) for t in range(2)
    ]
    own_first = lax.axis_index("tensor") == 0
    straight = jnp.concatenate(small, axis=1)
    turned = jnp.concatenate(small[::-1], axis=1)
    vecs[0:6, :] = jnp.where(own_first, straight, turned)[0:6]
    vecs[6:8, :] = straight[6:8]
    per = dm.fh // dm.width
    for t in range(2):
        up = jnp.concatenate([extra[t, f].astype(F32)[8:9, 0:up_share] for f in range(dm.shards)], axis=1)
        for j in range(per):
            vecs[8 + t * per + j : 9 + t * per + j, :] = up[:, j * dm.width : (j + 1) * dm.width]

    def weights_ready():
        for copy in late:
            copy.wait()

    output = layer_forward(dm, rows[...], w, vecs, st, False, weights_ready)
    for m in range(2):
        out[m, 0] = image(dm, output, m).astype(BF)


def live_of(count_ref, m):
    return (lax.axis_index("tensor") < count_ref[m, 0]).astype(F32)


def ring_slots(dm, ring):
    if not ring:
        return range(dm.shards)
    place = picked(RING_PLACE, lax.axis_index("fsdp"))
    return [lax.rem(RING_PLACE[f] + NEAR + dm.shards - place, dm.shards) for f in range(dm.shards)]


def kernel_second(dm, count_ref, tokens, h1, out_grad, w, vecs, acts, grad_in, *refs):
    st, refs = named(dm.state_shapes(), refs)
    ct, refs = named(dm.cotangent_shapes(), refs)
    work, _ = named(dm.work_shapes(), refs)
    rows = work["rows"]
    last = lax.axis_index("section") != 0

    @pl.when(jnp.logical_not(last))
    def _():
        spread(dm, rows, lambda m: tokens[m, 0].astype(F32))

    @pl.when(last)
    def _():
        spread(dm, rows, lambda m: h1[m, 0].astype(F32))

    output = layer_forward(dm, rows[...], w, vecs, st, True)
    for m in range(2):
        acts[m, 0] = (image(dm, output, m) * live_of(count_ref, m)).astype(BF)

    @pl.when(last)
    def _():
        spread(dm, rows, lambda m: out_grad[m, 0].astype(F32) * live_of(count_ref, m))
        grad = layer_backward(dm, rows[...], w, vecs, st, ct, work)
        for m in range(2):
            grad_in[m, 0] = image(dm, grad, m).astype(BF)


def kernel_third(dm, ring, incoming, w, vecs, own, *refs):
    st, refs = named(dm.state_shapes(), refs)
    given, refs = named(dm.cotangent_shapes(), refs)
    grad_in, grad_own, grad_other, *refs = refs
    ct, refs = named(dm.cotangent_shapes(), refs)
    work, _ = named(dm.work_shapes(), refs)
    rows = work["rows"]
    last = lax.axis_index("section") != 0

    @pl.when(jnp.logical_not(last))
    def _():
        spread(dm, rows, lambda m: incoming[m, 0].astype(F32))
        grad = layer_backward(dm, rows[...], w, vecs, st, ct, work)
        for m in range(2):
            grad_in[m, 0] = image(dm, grad, m).astype(BF)

    @pl.when(last)
    def _():
        grad_in[...] = own[...]
        for name in ct:
            ct[name][...] = given[name][...]

    parameter_grads(dm, st, ct, (grad_own, grad_other), ring_slots(dm, ring))


def kernel_unpack(dm, *refs):
    terms, (g_qkv, g_out, g_up, g_down, g_head, g_upb, g_gain, g_shift) = refs[:-8], refs[-8:]
    half, fh = dm.half, dm.fh

    def total(rows, lo, count):
        return sum(ref[rows, lo : lo + count].astype(F32) for ref in terms)

    every = slice(None)
    for k in range(3):
        g_qkv[k] = total(every, k * half, half)
    g_out[...] = total(every, dm.o_out, half)
    g_up[...] = total(every, dm.o_up, fh)
    g_down[...] = total(every, dm.o_down, fh)
    ext = total(slice(0, 16), dm.cols, EXT)
    share, up_share = half // dm.shards, fh // dm.shards
    g_gain[0] = ext[0:2, 0:share]
    g_shift[0] = ext[2:6, 0:share]
    g_head[0] = ext[6:8, 0:share]
    g_upb[...] = ext[8:9, 0:up_share]


VM = pl.BlockSpec(memory_space=pltpu.VMEM)
AN = pl.BlockSpec(memory_space=pl.ANY)
SM = pl.BlockSpec(memory_space=pltpu.SMEM)


def call(kernel, ins, outs, args, scratch=(), limit=16):
    return pl.pallas_call(
        kernel,
        in_specs=ins,
        out_specs=[VM] * len(outs),
        out_shape=[jax.ShapeDtypeStruct(s, d) for s, d in outs],
        scratch_shapes=list(scratch),
        compiler_params=pltpu.CompilerParams(vmem_limit_bytes=limit * 2**20),
    )(*args)


def shifted(value, cycle, step):
    count = len(cycle)
    return lax.ppermute(value, "fsdp", [(cycle[i], cycle[(i + step) % count]) for i in range(count)])


def gather_ring(block, cycle):
    count = len(cycle)
    ahead = behind = block
    found, layout = [block], [(0, 0)]
    for step in range(1, count // 2):
        ahead, behind = shifted(ahead, cycle, 1), shifted(behind, cycle, -1)
        found += [ahead, behind]
        layout += [(-step, 0), (step, 0)]
    cut = block.shape[1] // 256 * 128
    found += [shifted(ahead[:, :cut], cycle, 1), shifted(behind[:, cut:], cycle, -1)]
    layout += [(-(count // 2), 0), (count // 2, cut)]
    return found, layout


def both_ways(ahead, behind, cycle):
    ahead, behind = lax.optimization_barrier((ahead, behind))
    return lax.optimization_barrier((shifted(ahead, cycle, 1), shifted(behind, cycle, -1)))


def reduce_ring(own, other, cycle, swap):
    count = len(cycle)
    far = count // 2
    cut = own.shape[2] // 256 * 128
    split = NEAR + far - 1
    far_part = lax.ppermute(other[split:], "tensor", swap)
    near_part = lax.ppermute(other[:split], "tensor", swap)

    def part(offset, lo=0, hi=None, *more):
        slot = (offset + NEAR) % count
        given = far_part[slot - split] if slot >= split else near_part[slot]
        terms = (own[slot][:, lo:hi], given[:, lo:hi]) + more
        return sum(v.astype(F32) for v in terms).astype(BF)

    low, high = both_ways(part(far, 0, cut), part(far, cut), cycle)
    step = far - 1
    ahead = jnp.concatenate([part(step, 0, cut, low), part(step, cut)], axis=1)
    behind = jnp.concatenate([part(-step, 0, cut), part(-step, cut, None, high)], axis=1)
    left, right = both_ways(ahead, behind, cycle)
    for step in range(far - 2, 0, -1):
        ahead, behind = part(step, 0, None, left), part(-step, 0, None, right)
        left, right = both_ways(ahead, behind, cycle)
    return own[NEAR], near_part[NEAR], left, right


def per_device(tokens, out_grad, image_count, w_qkv, w_out, w_up, w_down, head_bias, up_bias, gains, shifts):
    seq, width = tokens.shape[2:]
    shards = lax.axis_size("fsdp")
    ring = shards == len(GRID_RING)
    hidden = w_up.shape[2] * 2
    dm = Dims(seq, width, hidden, len(GRID_RING))
    block = width // dm.shards
    swap = [(0, 1), (1, 0)]
    vectors = (head_bias, up_bias, gains, shifts)
    small = jnp.concatenate([gains[0], shifts[0], head_bias[0]], axis=0)
    if ring:
        ext = jnp.concatenate(
            [
                jnp.pad(small, ((0, 0), (0, EXT - small.shape[1]))),
                jnp.pad(up_bias, ((0, block - 9), (0, EXT - up_bias.shape[1]))),
            ],
            axis=0,
        )
        packed = jnp.concatenate(
            [w_qkv[0, :, 0], w_qkv[0, :, 1], w_qkv[0, :, 2], w_out[0].T, w_up[0], w_down[0].T, ext], axis=1
        )
        found, layout = gather_ring(packed, GRID_RING)
    else:
        rows = jnp.concatenate([w_qkv[0].reshape(w_qkv.shape[1], -1), w_out[0].T, w_up[0], w_down[0].T], axis=1)
        rows = lax.all_gather(rows, "fsdp", axis=0, tiled=True)
        small = lax.all_gather(small, "fsdp", axis=1, tiled=True)
        up = lax.all_gather(up_bias, "fsdp", axis=1, tiled=True)
        small = jnp.moveaxis(small.reshape(8, dm.shards, -1), 1, 0)
        ext = jnp.concatenate(
            [
                jnp.pad(small, ((0, 0), (0, 0), (0, EXT - small.shape[2]))),
                jnp.pad(
                    up.reshape(dm.shards, 1, -1), ((0, 0), (0, block - 9), (0, EXT - up.shape[1] // dm.shards))
                ),
            ],
            axis=1,
        )
        rows = jnp.concatenate([rows, ext.reshape(width, EXT)], axis=1)
        found = [rows[i * block : (i + 1) * block] for i in range(dm.shards)]
        layout = [(i, 0) for i in range(dm.shards)]
    others = [lax.ppermute(b, "tensor", swap) for b in found]
    states = dm.state_shapes()
    cotangents = dm.cotangent_shapes()
    shape = tokens.shape
    buffers = lambda shapes: [pltpu.VMEM(*v) for v in shapes]
    work = buffers(dm.work_shapes().values())
    w, vecs, low0 = call(
        functools.partial(kernel_first, dm, layout, ring),
        [VM] + [AN] * (2 * len(found)),
        [((2, width, dm.cols), BF), ((16, width), F32), (shape, BF)],
        (tokens,) + tuple(found) + tuple(others),
        scratch=buffers([states["proj"], states["probs"], states["mixed"], ((dm.rows, width), F32)])
        + [pltpu.VMEM((2, dm.shards, block, EXT), BF), pltpu.SemaphoreType.DMA((3, 2 * len(found)))],
    )
    h1 = lax.ppermute(low0, "section", [(0, 1)])
    kept = list(states.values()) + list(cotangents.values())
    acts, grad1, *kept = call(
        functools.partial(kernel_second, dm),
        [SM] + [VM] * 5,
        [(shape, BF), (shape, BF)] + kept,
        (image_count, tokens, h1, out_grad, w, vecs),
        scratch=work,
    )
    incoming = lax.ppermute(grad1, "section", [(1, 0)])
    in_grads, own, other = call(
        functools.partial(kernel_third, dm, ring),
        [VM] * (4 + len(kept)),
        [(shape, BF)] + [((dm.shards, block, dm.packed), BF)] * 2,
        (incoming, w, vecs, grad1) + tuple(kept),
        scratch=buffers(cotangents.values()) + work,
    )
    if ring:
        terms = reduce_ring(own, other, GRID_RING, swap)
        shapes = [(3, block, dm.half), (block, dm.half), (block, dm.fh), (block, dm.fh)] + [v.shape for v in vectors]
        g_qkv, g_out, g_up, g_down, *small = call(
            functools.partial(kernel_unpack, dm), [VM] * len(terms), [(v, F32) for v in shapes], terms
        )
        grads = [jnp.transpose(g_qkv, (1, 0, 2))[None], g_out.T[None], g_up[None], g_down.T[None], *small]
    else:
        half = dm.half
        mine = own.astype(F32) + lax.ppermute(other, "tensor", swap).astype(F32)
        mine = mine.reshape(width, dm.packed)
        body = lax.psum_scatter(mine[:, : dm.cols], "fsdp", scatter_dimension=0, tiled=True)
        share, up_share = half // dm.shards, dm.fh // dm.shards
        ext = mine[:, dm.cols :].reshape(dm.shards, block, EXT)
        small = jnp.moveaxis(ext[:, 0:8, 0:share], 0, 1).reshape(8, half)
        small = lax.psum_scatter(small, "fsdp", scatter_dimension=1, tiled=True)
        up = lax.psum_scatter(ext[:, 8, 0:up_share].reshape(-1), "fsdp", scatter_dimension=0, tiled=True)
        grads = [
            body[:, : 3 * half].reshape(w_qkv.shape),
            body[:, dm.o_out : dm.o_up].T[None],
            body[:, dm.o_up : dm.o_down][None],
            body[:, dm.o_down :].T[None],
            small[6:8][None],
            up[None],
            small[0:2][None],
            small[2:6][None],
        ]
    return (acts[None], in_grads[None], *grads)


def solution(mesh):
    both = ("tensor", "fsdp")
    params = (
        P("section", "fsdp", None, "tensor"),
        P("section", "tensor", "fsdp"),
        P("section", "fsdp", "tensor"),
        P("section", "tensor", "fsdp"),
        P("section", None, both),
        P("section", both),
        P("section", None, both),
        P("section", None, both),
    )
    images = P(None, ("fsdp", "tensor"), None, None)
    layered = P("section", None, ("fsdp", "tensor"), None, None)
    return jax.shard_map(
        per_device,
        mesh=mesh,
        in_specs=(images, images, P(None, "fsdp")) + params,
        out_specs=(layered, layered) + params,
        check_vma=False,
    )
```

```python
import functools
import math

import jax
import jax.numpy as jnp
from jax import lax
from jax.experimental import pallas as pl
from jax.experimental.pallas import tpu as pltpu
from jax.sharding import PartitionSpec as P

HD = 64
EPS = 1e-06
INV_ROOT_TWO = 0.7071067811865476
INV_ROOT_TWO_PI = 0.3989422804014327
SCALE = 1.0 / math.sqrt(HD)
BF = jnp.bfloat16
F32 = jnp.float32
GRID_RING = (0, 1, 3, 5, 7, 6, 4, 2)
RING_PLACE = tuple(GRID_RING.index(i) for i in range(len(GRID_RING)))
KEPT_OWN = (7, 6, 4, 2, 0, 9, 11, 13)
KEPT_OTHER = (15, 5, 3, 1, 8, 10, 12, 14)
ROW_STEP = 88
EXT = 128


def dot(a, b, dims):
    return lax.dot_general(a, b, (dims, ((), ())), preferred_element_type=F32)


def nn(a, b):
    return dot(a, b, ((1,), (0,)))


def nt(a, b):
    return dot(a, b, ((1,), (1,)))


def tn(a, b):
    return dot(a, b, ((0,), (0,)))


def norm(value):
    mean = jnp.mean(value, axis=-1, keepdims=True)
    centred = value - mean
    var = jnp.mean(centred * centred, axis=-1, keepdims=True)
    factor = lax.rsqrt(var + EPS)
    return centred * factor, factor


def norm_back(grad, unit, factor, gain):
    scaled = grad * gain
    plain = jnp.mean(scaled, axis=-1, keepdims=True)
    along = jnp.mean(scaled * unit, axis=-1, keepdims=True)
    return (scaled - plain - unit * along) * factor


def picked(options, index):
    value = jnp.int32(options[0])
    for i in range(1, len(options)):
        value = jnp.where(index == i, jnp.int32(options[i]), value)
    return value


class Dims:
    def __init__(self, seq, width, hidden, shards):
        self.seq, self.width, self.hidden, self.shards = seq, width, hidden, shards
        self.half = width // 2
        self.fh = hidden // 2
        self.heads = self.half // HD
        self.o_out = 3 * self.half
        self.o_up = self.o_out + self.half
        self.o_down = self.o_up + self.fh
        self.cols = self.o_down + self.fh
        self.packed = self.cols + EXT
        self.rows = 2 * ROW_STEP
        self.o_vecs = width
        self.o_image = width + 16
        self.o_grad = self.o_image + 96
        self.w_rows = self.o_grad + 96

    def state_shapes(self):
        r, w = self.rows, self.width
        return dict(
            proj=((2, r, 3 * self.half), F32),
            probs=((4 * self.heads, ROW_STEP, ROW_STEP), F32),
            mixed=((2, r, self.half), F32),
            unit_one=((r, w), F32),
            factors=((2, r, 1), F32),
            first=((r, w), BF),
            unit_two=((r, w), F32),
            second=((r, w), BF),
            slope=((2, r, self.fh), F32),
            active=((2, r, self.fh), BF),
        )

    def cotangent_shapes(self):
        r, w = self.rows, self.width
        return dict(
            branch=((r, w), BF),
            hidden=((2, r, self.fh), BF),
            attn=((r, w), BF),
            proj=((2, r, 3 * self.half), F32),
            vecs=((16, w), F32),
        )

    def work_shapes(self):
        return dict(
            rows=((self.rows, self.width), F32),
            mixed=((2, self.rows, self.half), F32),
            scores=((4 * self.heads, ROW_STEP, ROW_STEP), F32),
        )

    def cells(self):
        for t in range(2):
            for m in range(2):
                for h in range(self.heads):
                    rows = slice(m * ROW_STEP, (m + 1) * ROW_STEP)
                    yield (t * 2 + m) * self.heads + h, t, rows, h * HD


def forward_attention(dm, state, w, vecs, st, keep):
    half = dm.half
    unit, factor = norm(state)
    first = (unit * vecs[0:1, :] + vecs[2:3, :]).astype(BF)
    if keep:
        st["unit_one"][...] = unit
        st["factors"][0] = factor
        st["first"][...] = first
    proj, mixed = st["proj"], st["mixed"]
    for t in range(2):
        value = nn(first, w[t, 0 : dm.width, 0 : 3 * half])
        proj[t, :, 0:half] = value[:, 0:half] + vecs[6:7, t * half : (t + 1) * half]
        proj[t, :, half : 2 * half] = value[:, half : 2 * half]
        proj[t, :, 2 * half :] = value[:, 2 * half :] + vecs[7:8, t * half : (t + 1) * half]
    for i, t, rows, c in dm.cells():
        query, keys = proj[t, rows, c : c + HD], proj[t, rows, half + c : half + c + HD]
        st["probs"][i] = nt(query.astype(BF), keys.astype(BF))
    scores = st["probs"][...] * SCALE
    column = lax.broadcasted_iota(jnp.int32, scores.shape, 2)
    scores = jnp.where(column < dm.seq, scores, -1e30)
    expo = jnp.exp(scores - jnp.max(scores, axis=-1, keepdims=True))
    st["probs"][...] = expo * (1.0 / jnp.sum(expo, axis=-1, keepdims=True))
    for i, t, rows, c in dm.cells():
        values = proj[t, rows, 2 * half + c : 2 * half + c + HD]
        mixed[t, rows, c : c + HD] = nn(st["probs"][i].astype(BF), values.astype(BF))
    resid = state + vecs[3:4, :]
    for t in range(2):
        resid += nt(mixed[t].astype(BF), w[t, 0 : dm.width, dm.o_out : dm.o_out + half])
    return resid


def forward_mlp(dm, resid, w, vecs, st, keep):
    fh = dm.fh
    unit, factor = norm(resid)
    second = (unit * vecs[1:2, :] + vecs[4:5, :]).astype(BF)
    if keep:
        st["unit_two"][...] = unit
        st["factors"][1] = factor
        st["second"][...] = second
    output = resid + vecs[5:6, :]
    per = fh // dm.width
    for t in range(2):
        bias = jnp.concatenate([vecs[8 + t * per + j : 9 + t * per + j, :] for j in range(per)], axis=1)
        hidden = nn(second, w[t, 0 : dm.width, dm.o_up : dm.o_up + fh]) + bias
        curve = 0.5 * (1.0 + lax.erf(hidden * INV_ROOT_TWO))
        active = (hidden * curve).astype(BF)
        if keep:
            st["slope"][t] = curve + hidden * jnp.exp(-0.5 * hidden * hidden) * INV_ROOT_TWO_PI
            st["active"][t] = active
        output += nt(active, w[t, 0 : dm.width, dm.o_down : dm.o_down + fh])
    return output


def total_rows(value):
    return jnp.sum(value, axis=0, keepdims=True)


def layer_backward(dm, grad, w, vecs, st, ct, work):
    half, fh = dm.half, dm.fh
    low = grad.astype(BF)
    ct["branch"][...] = low
    shift_branch = total_rows(low.astype(F32))
    per = fh // dm.width
    grad_second = None
    for t in range(2):
        raw = nn(low, w[t, 0 : dm.width, dm.o_down : dm.o_down + fh]) * st["slope"][t]
        up_bias = total_rows(raw)
        for j in range(per):
            ct["vecs"][8 + t * per + j : 9 + t * per + j, :] = up_bias[:, j * dm.width : (j + 1) * dm.width]
        grad_hidden = raw.astype(BF)
        ct["hidden"][t] = grad_hidden
        part = nt(grad_hidden, w[t, 0 : dm.width, dm.o_up : dm.o_up + fh])
        grad_second = part if grad_second is None else grad_second + part
    unit = st["unit_two"][...]
    gain_two, shift_two = total_rows(grad_second * unit), total_rows(grad_second)
    grad_resid = grad + norm_back(grad_second, unit, st["factors"][1], vecs[1:2, :])
    low = grad_resid.astype(BF)
    ct["attn"][...] = low
    shift_attn = total_rows(low.astype(F32))
    proj, gproj, gmix, scores = st["proj"], ct["proj"], work["mixed"], work["scores"]
    for t in range(2):
        gmix[t] = nn(low, w[t, 0 : dm.width, dm.o_out : dm.o_out + half])
    for i, t, rows, c in dm.cells():
        values = proj[t, rows, 2 * half + c : 2 * half + c + HD].astype(BF)
        gm = gmix[t, rows, c : c + HD].astype(BF)
        scores[i] = nt(gm, values)
        gproj[t, rows, 2 * half + c : 2 * half + c + HD] = tn(st["probs"][i].astype(BF), gm)
    probs, gp = st["probs"][...], scores[...]
    scores[...] = probs * (gp - jnp.sum(gp * probs, axis=-1, keepdims=True)) * SCALE
    for i, t, rows, c in dm.cells():
        query = proj[t, rows, c : c + HD].astype(BF)
        keys = proj[t, rows, half + c : half + c + HD].astype(BF)
        gs = scores[i].astype(BF)
        gproj[t, rows, c : c + HD] = nn(gs, keys)
        gproj[t, rows, half + c : half + c + HD] = tn(gs, query)
    grad_first = None
    for t in range(2):
        ct["vecs"][6:7, t * half : (t + 1) * half] = total_rows(gproj[t, :, 0:half])
        ct["vecs"][7:8, t * half : (t + 1) * half] = total_rows(gproj[t, :, 2 * half :])
        part = nt(gproj[t].astype(BF), w[t, 0 : dm.width, 0 : 3 * half])
        grad_first = part if grad_first is None else grad_first + part
    unit = st["unit_one"][...]
    gain_one, shift_one = total_rows(grad_first * unit), total_rows(grad_first)
    for i, v in enumerate((gain_one, gain_two, shift_one, shift_attn, shift_two, shift_branch)):
        ct["vecs"][i : i + 1, :] = v
    return grad_resid + norm_back(grad_first, unit, st["factors"][0], vecs[0:1, :])


def parameter_grads(dm, st, ct, grads, slots):
    half, fh = dm.half, dm.fh
    block = dm.width // dm.shards

    def keep(t, column, value):
        for f in range(dm.shards):
            rows = value[f * block : (f + 1) * block].astype(BF)
            grads[slots[t][f], :, column : column + value.shape[1]] = rows

    for t in range(2):
        keep(t, dm.o_down, tn(ct["branch"][...], st["active"][t]))
        keep(t, dm.o_up, tn(st["second"][...], ct["hidden"][t]))
        keep(t, dm.o_out, tn(ct["attn"][...], st["mixed"][t].astype(BF)))
        keep(t, 0, tn(st["first"][...], ct["proj"][t].astype(BF)))
    own_first = lax.axis_index("tensor") == 0
    plain = ct["vecs"][0:6, :]
    turned = jnp.concatenate([plain[:, half:], plain[:, 0:half]], axis=1)
    plain = jnp.where(own_first, plain, turned)
    share, up_share = half // dm.shards, fh // dm.shards
    per = fh // dm.width
    for t in range(2):
        stack = jnp.concatenate([plain, ct["vecs"][6:8, :]], axis=0)[:, t * half : (t + 1) * half]
        up = jnp.concatenate([ct["vecs"][8 + t * per + j : 9 + t * per + j, :] for j in range(per)], axis=1)
        for f in range(dm.shards):
            piece = jnp.concatenate([stack[:, f * share : (f + 1) * share], jnp.zeros((8, EXT - share), F32)], axis=1)
            up_piece = up[:, f * up_share : (f + 1) * up_share]
            up_piece = jnp.concatenate([up_piece, jnp.zeros((1, EXT - up_share), F32)], axis=1)
            piece = jnp.concatenate([piece, up_piece, jnp.zeros((block - 9, EXT), F32)], axis=0)
            grads[slots[t][f], :, dm.cols :] = piece.astype(BF)


def spread(dm, ref, get):
    pad = jnp.zeros((ROW_STEP - dm.seq, dm.width), F32)
    for m in range(2):
        ref[m * ROW_STEP : m * ROW_STEP + dm.seq, :] = get(m)
        ref[m * ROW_STEP + dm.seq : (m + 1) * ROW_STEP, :] = pad


def image(dm, value, m):
    return value[m * ROW_STEP : m * ROW_STEP + dm.seq, :]


def named(shapes, refs):
    return dict(zip(shapes, refs)), refs[len(shapes) :]


def kernel_first(dm, layout, ring, count_ref, tokens, out_grad, *refs):
    pieces, refs = refs[:-8], refs[-8:]
    w, out, proj, probs, mixed, rows, extra, sems = refs
    st = dict(proj=proj, probs=probs, mixed=mixed)
    block = dm.width // dm.shards
    early, late = [], []
    if ring:
        place = picked(RING_PLACE, lax.axis_index("fsdp"))
    for n, (t, array, row, offset, start, stop) in enumerate(layout):
        if ring:
            owner = jnp.where(
                lax.axis_index("tensor") == 0,
                picked([GRID_RING[(p + offset) % dm.shards] for p in range(dm.shards)], place),
                picked([GRID_RING[(p - offset) % dm.shards] for p in range(dm.shards)], place),
            )
            where = pl.ds(pl.multiple_of(owner * block, 16), block)
        else:
            owner = offset
            where = pl.ds(offset * block, block)
        bounds = (0, dm.o_up, dm.cols, dm.packed)
        for j in range(3):
            lo, hi = max(start, bounds[j]), min(stop, bounds[j + 1])
            if lo < hi:
                target = extra.at[t, owner] if j == 2 else w.at[t, where, pl.ds(lo, hi - lo)]
                source = pieces[array].at[pl.ds(row, block), pl.ds(lo - start, hi - lo)]
                copy = pltpu.make_async_copy(source, target, sems.at[j, n])
                (late if j == 1 else early).append(copy)
    for copy in early + late:
        copy.start()
    live = [live_of(count_ref, m) for m in range(2)]

    def put(start):
        for m in range(2):
            value = jnp.concatenate([rows[m * ROW_STEP : (m + 1) * ROW_STEP, :], jnp.zeros((8, dm.width), F32)], axis=0)
            w[m, start : start + 96, 0 : dm.width] = value.astype(BF)

    value = out_grad[...].astype(F32)
    spread(dm, rows, lambda m: value[:, m, :] * live[m])
    put(dm.o_grad)
    value = tokens[...].astype(F32)
    spread(dm, rows, lambda m: value[:, m, :])
    put(dm.o_image)
    for copy in early:
        copy.wait()
    share, up_share = dm.half // dm.shards, dm.fh // dm.shards
    small = [
        jnp.concatenate([extra[t, f].astype(F32)[0:8, 0:share] for f in range(dm.shards)], axis=1) for t in range(2)
    ]
    own_first = lax.axis_index("tensor") == 0
    straight = jnp.concatenate(small, axis=1)
    turned = jnp.concatenate(small[::-1], axis=1)
    vecs = [jnp.where(own_first, straight, turned)[0:6], straight[6:8]]
    per = dm.fh // dm.width
    for t in range(2):
        up = jnp.concatenate([extra[t, f].astype(F32)[8:9, 0:up_share] for f in range(dm.shards)], axis=1)
        vecs += [up[:, j * dm.width : (j + 1) * dm.width] for j in range(per)]
    vecs += [jnp.full((1, dm.width), v, F32) for v in live]
    vecs.append(jnp.zeros((6 - 2 * per, dm.width), F32))
    vecs = jnp.concatenate(vecs, axis=0)
    w[0, dm.o_vecs : dm.o_image, 0 : dm.width] = vecs.astype(BF)
    used = lax.axis_index("section") == 0

    @pl.when(used)
    def _():
        rows[...] = forward_attention(dm, rows[...], w, vecs, st, False)

    for copy in late:
        copy.wait()

    @pl.when(used)
    def _():
        output = forward_mlp(dm, rows[...], w, vecs, st, False)
        for m in range(2):
            out[m, 0] = image(dm, output, m).astype(BF)


def vectors_of(dm, w):
    return w[0, dm.o_vecs : dm.o_image, 0 : dm.width].astype(F32)


def live_of(count_ref, m):
    return (lax.axis_index("tensor") < count_ref[m, 0]).astype(F32)


def ring_slots(dm, ring):
    if not ring:
        return [range(t * dm.shards, (t + 1) * dm.shards) for t in range(2)]
    place = picked(RING_PLACE, lax.axis_index("fsdp"))
    found = [[], []]
    for p in RING_PLACE:
        ahead = jnp.where(lax.axis_index("tensor") == 0, p - place, place - p)
        ahead = lax.rem(ahead + dm.shards, dm.shards)
        found[0].append(picked(KEPT_OWN, ahead))
        found[1].append(picked(KEPT_OTHER, ahead))
    return found


def kernel_second(dm, h1, w, acts, grad_in, *refs):
    st, refs = named(dm.state_shapes(), refs)
    ct, refs = named(dm.cotangent_shapes(), refs)
    work, _ = named(dm.work_shapes(), refs)
    rows = work["rows"]
    last = lax.axis_index("section") != 0

    def take(start):
        for m in range(2):
            value = w[m, start : start + 96, 0 : dm.width].astype(F32)
            rows[m * ROW_STEP : (m + 1) * ROW_STEP, :] = value[0:ROW_STEP]

    @pl.when(jnp.logical_not(last))
    def _():
        take(dm.o_image)

    @pl.when(last)
    def _():
        spread(dm, rows, lambda m: h1[m, 0].astype(F32))

    vecs = vectors_of(dm, w)
    output = forward_mlp(dm, forward_attention(dm, rows[...], w, vecs, st, True), w, vecs, st, True)
    for m in range(2):
        acts[m, 0] = (image(dm, output, m) * vecs[12 + m : 13 + m]).astype(BF)

    @pl.when(last)
    def _():
        take(dm.o_grad)
        grad = layer_backward(dm, rows[...], w, vecs, st, ct, work)
        for m in range(2):
            grad_in[m, 0] = image(dm, grad, m).astype(BF)


def kernel_third(dm, ring, incoming, w, own, *refs):
    st, refs = named(dm.state_shapes(), refs)
    given, refs = named(dm.cotangent_shapes(), refs)
    grad_in, grads, *refs = refs
    ct, refs = named(dm.cotangent_shapes(), refs)
    work, _ = named(dm.work_shapes(), refs)
    rows = work["rows"]
    last = lax.axis_index("section") != 0

    @pl.when(jnp.logical_not(last))
    def _():
        spread(dm, rows, lambda m: incoming[m, 0].astype(F32))
        grad = layer_backward(dm, rows[...], w, vectors_of(dm, w), st, ct, work)
        for m in range(2):
            grad_in[m, 0] = image(dm, grad, m).astype(BF)

    @pl.when(last)
    def _():
        grad_in[...] = own[...]
        for name in ct:
            ct[name][...] = given[name][...]

    parameter_grads(dm, st, ct, grads, ring_slots(dm, ring))


def kernel_unpack(dm, *refs):
    terms, (g_qkv, g_out, g_up, g_down, g_head, g_upb, g_gain, g_shift) = refs[:-8], refs[-8:]
    half, fh = dm.half, dm.fh

    def total(rows, lo, count):
        return sum(ref[rows, lo : lo + count].astype(F32) for ref in terms)

    every = slice(None)
    for k in range(3):
        g_qkv[k] = total(every, k * half, half)
    g_out[...] = total(every, dm.o_out, half)
    g_up[...] = total(every, dm.o_up, fh)
    g_down[...] = total(every, dm.o_down, fh)
    ext = total(slice(0, 16), dm.cols, EXT)
    share, up_share = half // dm.shards, fh // dm.shards
    g_gain[0] = ext[0:2, 0:share]
    g_shift[0] = ext[2:6, 0:share]
    g_head[0] = ext[6:8, 0:share]
    g_upb[...] = ext[8:9, 0:up_share]


VM = pl.BlockSpec(memory_space=pltpu.VMEM)
AN = pl.BlockSpec(memory_space=pl.ANY)
SM = pl.BlockSpec(memory_space=pltpu.SMEM)


def call(kernel, ins, outs, args, scratch=(), limit=16):
    return pl.pallas_call(
        kernel,
        in_specs=ins,
        out_specs=[VM] * len(outs),
        out_shape=[jax.ShapeDtypeStruct(s, d) for s, d in outs],
        scratch_shapes=list(scratch),
        compiler_params=pltpu.CompilerParams(vmem_limit_bytes=limit * 2**20),
    )(*args)


def onward(value, cycle):
    count = len(cycle)
    route = []
    for i in range(count):
        route.append((cycle[i], cycle[(i + 1) % count]))
        route.append((count + cycle[i], count + cycle[(i - 1) % count]))
    return lax.ppermute(value, ("tensor", "fsdp"), route)


def gather_ring(block, cycle, swap):
    far = len(cycle) // 2
    own, other = [block], [lax.ppermute(block, "tensor", swap)]
    for step in range(far):
        own.append(onward(own[-1], cycle))
        if step + 1 < far:
            other.append(onward(other[-1], cycle))
    found, places = own + other, [(0, -s) for s in range(far + 1)] + [(1, -s) for s in range(far)]
    for t, values in ((1, own), (0, other)):
        for step in range(1, len(values)):
            found.append(lax.ppermute(values[step], "tensor", swap))
            places.append((t, step))
    layout = [(t, i, 0, offset, 0, block.shape[1]) for i, (t, offset) in enumerate(places)]
    return found, layout


def reduce_ring(blocks, cycle, swap):
    count = len(cycle)
    early = 3
    first = lax.ppermute(blocks[count : count + early], "tensor", swap)
    later = lax.ppermute(blocks[count + early :], "tensor", swap)

    def part(i, *more):
        given = first[i] if i < early else later[i - early]
        return sum(v.astype(F32) for v in (blocks[i], given) + more).astype(BF)

    def after(value, sent):
        return lax.optimization_barrier((value, sent))[0]

    own = onward(part(0), cycle)
    sent = part(1)
    other = onward(sent, cycle)
    for i in range(2, count, 2):
        sent = part(i, after(own, sent))
        own = onward(sent, cycle)
        if i + 1 < count - 1:
            sent = part(i + 1, after(other, sent))
            other = onward(sent, cycle)
    other = lax.ppermute(other, "tensor", swap)
    return blocks[count - 1], later[count - 1 - early], own, other


def per_device(tokens, out_grad, image_count, w_qkv, w_out, w_up, w_down, head_bias, up_bias, gains, shifts):
    seq, width = tokens.shape[2:]
    shards = lax.axis_size("fsdp")
    ring = shards == len(GRID_RING)
    hidden = w_up.shape[2] * 2
    dm = Dims(seq, width, hidden, len(GRID_RING))
    block = width // dm.shards
    swap = [(0, 1), (1, 0)]
    vectors = (head_bias, up_bias, gains, shifts)
    if ring:
        places = [(w_qkv[0, :, k], 0, k * dm.half) for k in range(3)]
        places += [(w_out[0].T, 0, dm.o_out), (w_up[0], 0, dm.o_up), (w_down[0].T, 0, dm.o_down)]
        places += [(v, r, dm.cols) for v, r in ((gains[0], 0), (shifts[0], 2), (head_bias[0], 6), (up_bias, 8))]
        packed = sum(
            jnp.pad(v, ((r, block - r - v.shape[0]), (c, dm.packed - c - v.shape[1]))) for v, r, c in places
        )
        found, layout = gather_ring(packed, GRID_RING, swap)
    else:
        rows = jnp.concatenate([w_qkv[0].reshape(w_qkv.shape[1], -1), w_out[0].T, w_up[0], w_down[0].T], axis=1)
        rows = lax.all_gather(rows, "fsdp", axis=0, tiled=True)
        small = jnp.concatenate([gains[0], shifts[0], head_bias[0]], axis=0)
        small = lax.all_gather(small, "fsdp", axis=1, tiled=True)
        up = lax.all_gather(up_bias, "fsdp", axis=1, tiled=True)
        small = jnp.moveaxis(small.reshape(8, dm.shards, -1), 1, 0)
        ext = jnp.concatenate(
            [
                jnp.pad(small, ((0, 0), (0, 0), (0, EXT - small.shape[2]))),
                jnp.pad(
                    up.reshape(dm.shards, 1, -1), ((0, 0), (0, block - 9), (0, EXT - up.shape[1] // dm.shards))
                ),
            ],
            axis=1,
        )
        rows = jnp.concatenate([rows, ext.reshape(width, EXT)], axis=1)
        found = [rows, lax.ppermute(rows, "tensor", swap)]
        layout = [(t, t, i * block, i, 0, dm.packed) for t in range(2) for i in range(dm.shards)]
    states = dm.state_shapes()
    cotangents = dm.cotangent_shapes()
    shape = tokens.shape
    buffers = lambda shapes: [pltpu.VMEM(*v) for v in shapes]
    work = buffers(dm.work_shapes().values())
    w, low0 = call(
        functools.partial(kernel_first, dm, layout, ring),
        [SM, VM, VM] + [AN] * len(found),
        [((2, dm.w_rows, dm.cols), BF), (shape, BF)],
        (image_count,) + tuple(jnp.transpose(v[:, 0], (1, 0, 2)) for v in (tokens, out_grad)) + tuple(found),
        scratch=buffers([states["proj"], states["probs"], states["mixed"], ((dm.rows, width), F32)])
        + [pltpu.VMEM((2, dm.shards, block, EXT), BF), pltpu.SemaphoreType.DMA((3, len(layout)))],
    )
    h1 = lax.ppermute(low0, "section", [(0, 1)])
    kept = list(states.values()) + list(cotangents.values())
    acts, grad1, *kept = call(
        functools.partial(kernel_second, dm),
        [VM] * 2,
        [(shape, BF), (shape, BF)] + kept,
        (h1, w),
        scratch=work,
    )
    incoming = lax.ppermute(grad1, "section", [(1, 0)])
    in_grads, blocks = call(
        functools.partial(kernel_third, dm, ring),
        [VM] * (3 + len(kept)),
        [(shape, BF), ((2 * dm.shards, block, dm.packed), BF)],
        (incoming, w, grad1) + tuple(kept),
        scratch=buffers(cotangents.values()) + work,
    )
    if ring:
        terms = reduce_ring(blocks, GRID_RING, swap)
        shapes = [(3, block, dm.half), (block, dm.half), (block, dm.fh), (block, dm.fh)] + [v.shape for v in vectors]
        g_qkv, g_out, g_up, g_down, *small = call(
            functools.partial(kernel_unpack, dm), [VM] * len(terms), [(v, F32) for v in shapes], terms
        )
        grads = [jnp.transpose(g_qkv, (1, 0, 2))[None], g_out.T[None], g_up[None], g_down.T[None], *small]
    else:
        half = dm.half
        mine = blocks[: dm.shards].astype(F32)
        mine += lax.ppermute(blocks[dm.shards :], "tensor", swap).astype(F32)
        mine = mine.reshape(width, dm.packed)
        body = lax.psum_scatter(mine[:, : dm.cols], "fsdp", scatter_dimension=0, tiled=True)
        share, up_share = half // dm.shards, dm.fh // dm.shards
        ext = mine[:, dm.cols :].reshape(dm.shards, block, EXT)
        small = jnp.moveaxis(ext[:, 0:8, 0:share], 0, 1).reshape(8, half)
        small = lax.psum_scatter(small, "fsdp", scatter_dimension=1, tiled=True)
        up = lax.psum_scatter(ext[:, 8, 0:up_share].reshape(-1), "fsdp", scatter_dimension=0, tiled=True)
        grads = [
            body[:, : 3 * half].reshape(w_qkv.shape),
            body[:, dm.o_out : dm.o_up].T[None],
            body[:, dm.o_up : dm.o_down][None],
            body[:, dm.o_down :].T[None],
            small[6:8][None],
            up[None],
            small[0:2][None],
            small[2:6][None],
        ]
    return (acts[None], in_grads[None], *grads)


def solution(mesh):
    both = ("tensor", "fsdp")
    params = (
        P("section", "fsdp", None, "tensor"),
        P("section", "tensor", "fsdp"),
        P("section", "fsdp", "tensor"),
        P("section", "tensor", "fsdp"),
        P("section", None, both),
        P("section", both),
        P("section", None, both),
        P("section", None, both),
    )
    images = P(None, ("fsdp", "tensor"), None, None)
    layered = P("section", None, ("fsdp", "tensor"), None, None)
    return jax.shard_map(
        per_device,
        mesh=mesh,
        in_specs=(images, images, P(None, "fsdp")) + params,
        out_specs=(layered, layered) + params,
        check_vma=False,
    )
```

```python
import functools
import math

import jax
import jax.numpy as jnp
from jax import lax
from jax.experimental import pallas as pl
from jax.experimental.pallas import tpu as pltpu
from jax.sharding import PartitionSpec as P

HD = 64
EPS = 1e-06
INV_ROOT_TWO = 0.7071067811865476
INV_ROOT_TWO_PI = 0.3989422804014327
SCALE = 1.0 / math.sqrt(HD)
BF = jnp.bfloat16
F32 = jnp.float32
GRID_RING = (0, 1, 3, 5, 7, 6, 4, 2)
RING_PLACE = tuple(GRID_RING.index(i) for i in range(len(GRID_RING)))
KEPT_OWN = (7, 6, 4, 2, 0, 9, 11, 13)
KEPT_OTHER = (15, 5, 3, 1, 8, 10, 12, 14)
ROW_STEP = 88
EXT = 128


def dot(a, b, dims):
    return lax.dot_general(a, b, (dims, ((), ())), preferred_element_type=F32)


def nn(a, b):
    return dot(a, b, ((1,), (0,)))


def nt(a, b):
    return dot(a, b, ((1,), (1,)))


def tn(a, b):
    return dot(a, b, ((0,), (0,)))


def norm(value):
    mean = jnp.mean(value, axis=-1, keepdims=True)
    centred = value - mean
    var = jnp.mean(centred * centred, axis=-1, keepdims=True)
    factor = lax.rsqrt(var + EPS)
    return centred * factor, factor


def norm_back(grad, unit, factor, gain):
    scaled = grad * gain
    plain = jnp.mean(scaled, axis=-1, keepdims=True)
    along = jnp.mean(scaled * unit, axis=-1, keepdims=True)
    return (scaled - plain - unit * along) * factor


def picked(options, index):
    value = jnp.int32(options[0])
    for i in range(1, len(options)):
        value = jnp.where(index == i, jnp.int32(options[i]), value)
    return value


class Dims:
    def __init__(self, seq, width, hidden, shards):
        self.seq, self.width, self.hidden, self.shards = seq, width, hidden, shards
        self.half = width // 2
        self.fh = hidden // 2
        self.heads = self.half // HD
        self.o_out = 3 * self.half
        self.o_ext = self.o_out + self.half
        self.o_up = self.o_ext + EXT
        self.o_down = self.o_up + self.fh
        self.packed = self.o_down + self.fh
        self.rows = 2 * ROW_STEP
        self.o_vecs = width
        self.o_image = width + 16
        self.o_grad = self.o_image + 96
        self.w_rows = self.o_grad + 96

    def state_shapes(self):
        r, w = self.rows, self.width
        return dict(
            proj=((2, r, 3 * self.half), F32),
            probs=((4 * self.heads, ROW_STEP, ROW_STEP), F32),
            mixed=((2, r, self.half), F32),
            unit_one=((r, w), F32),
            factors=((2, r, 1), F32),
            first=((r, w), BF),
            unit_two=((r, w), F32),
            second=((r, w), BF),
            slope=((2, r, self.fh), F32),
            active=((2, r, self.fh), BF),
        )

    def cotangent_shapes(self):
        r, w = self.rows, self.width
        return dict(
            branch=((r, w), BF),
            hidden=((2, r, self.fh), BF),
            attn=((r, w), BF),
            proj=((2, r, 3 * self.half), F32),
            vecs=((16, w), F32),
        )

    def work_shapes(self):
        return dict(
            rows=((self.rows, self.width), F32),
            mixed=((2, self.rows, self.half), F32),
            scores=((4 * self.heads, ROW_STEP, ROW_STEP), F32),
        )

    def cells(self):
        for t in range(2):
            for m in range(2):
                for h in range(self.heads):
                    rows = slice(m * ROW_STEP, (m + 1) * ROW_STEP)
                    yield (t * 2 + m) * self.heads + h, t, rows, h * HD


def forward_attention(dm, state, w, vecs, st, keep):
    half = dm.half
    unit, factor = norm(state)
    first = (unit * vecs[0:1, :] + vecs[2:3, :]).astype(BF)
    if keep:
        st["unit_one"][...] = unit
        st["factors"][0] = factor
        st["first"][...] = first
    proj, mixed = st["proj"], st["mixed"]
    for t in range(2):
        value = nn(first, w[t, 0 : dm.width, 0 : 3 * half])
        proj[t, :, 0:half] = value[:, 0:half] + vecs[6:7, t * half : (t + 1) * half]
        proj[t, :, half : 2 * half] = value[:, half : 2 * half]
        proj[t, :, 2 * half :] = value[:, 2 * half :] + vecs[7:8, t * half : (t + 1) * half]
    for i, t, rows, c in dm.cells():
        query, keys = proj[t, rows, c : c + HD], proj[t, rows, half + c : half + c + HD]
        st["probs"][i] = nt(query.astype(BF), keys.astype(BF))
    scores = st["probs"][...] * SCALE
    column = lax.broadcasted_iota(jnp.int32, scores.shape, 2)
    scores = jnp.where(column < dm.seq, scores, -1e30)
    expo = jnp.exp(scores - jnp.max(scores, axis=-1, keepdims=True))
    st["probs"][...] = expo * (1.0 / jnp.sum(expo, axis=-1, keepdims=True))
    for i, t, rows, c in dm.cells():
        values = proj[t, rows, 2 * half + c : 2 * half + c + HD]
        mixed[t, rows, c : c + HD] = nn(st["probs"][i].astype(BF), values.astype(BF))
    resid = state + vecs[3:4, :]
    for t in range(2):
        resid += nt(mixed[t].astype(BF), w[t, 0 : dm.width, dm.o_out : dm.o_out + half])
    return resid


def forward_mlp(dm, resid, w, vecs, st, keep):
    fh = dm.fh
    unit, factor = norm(resid)
    second = (unit * vecs[1:2, :] + vecs[4:5, :]).astype(BF)
    if keep:
        st["unit_two"][...] = unit
        st["factors"][1] = factor
        st["second"][...] = second
    output = resid + vecs[5:6, :]
    per = fh // dm.width
    for t in range(2):
        bias = jnp.concatenate([vecs[8 + t * per + j : 9 + t * per + j, :] for j in range(per)], axis=1)
        hidden = nn(second, w[t, 0 : dm.width, dm.o_up : dm.o_up + fh]) + bias
        curve = 0.5 * (1.0 + lax.erf(hidden * INV_ROOT_TWO))
        active = (hidden * curve).astype(BF)
        if keep:
            st["slope"][t] = curve + hidden * jnp.exp(-0.5 * hidden * hidden) * INV_ROOT_TWO_PI
            st["active"][t] = active
        output += nt(active, w[t, 0 : dm.width, dm.o_down : dm.o_down + fh])
    return output


def total_rows(value):
    return jnp.sum(value, axis=0, keepdims=True)


def layer_backward(dm, grad, w, vecs, st, ct, work):
    half, fh = dm.half, dm.fh
    low = grad.astype(BF)
    ct["branch"][...] = low
    shift_branch = total_rows(low.astype(F32))
    per = fh // dm.width
    grad_second = None
    for t in range(2):
        raw = nn(low, w[t, 0 : dm.width, dm.o_down : dm.o_down + fh]) * st["slope"][t]
        up_bias = total_rows(raw)
        for j in range(per):
            ct["vecs"][8 + t * per + j : 9 + t * per + j, :] = up_bias[:, j * dm.width : (j + 1) * dm.width]
        grad_hidden = raw.astype(BF)
        ct["hidden"][t] = grad_hidden
        part = nt(grad_hidden, w[t, 0 : dm.width, dm.o_up : dm.o_up + fh])
        grad_second = part if grad_second is None else grad_second + part
    unit = st["unit_two"][...]
    gain_two, shift_two = total_rows(grad_second * unit), total_rows(grad_second)
    grad_resid = grad + norm_back(grad_second, unit, st["factors"][1], vecs[1:2, :])
    low = grad_resid.astype(BF)
    ct["attn"][...] = low
    shift_attn = total_rows(low.astype(F32))
    proj, gproj, gmix, scores = st["proj"], ct["proj"], work["mixed"], work["scores"]
    for t in range(2):
        gmix[t] = nn(low, w[t, 0 : dm.width, dm.o_out : dm.o_out + half])
    for i, t, rows, c in dm.cells():
        values = proj[t, rows, 2 * half + c : 2 * half + c + HD].astype(BF)
        gm = gmix[t, rows, c : c + HD].astype(BF)
        scores[i] = nt(gm, values)
        gproj[t, rows, 2 * half + c : 2 * half + c + HD] = tn(st["probs"][i].astype(BF), gm)
    probs, gp = st["probs"][...], scores[...]
    scores[...] = probs * (gp - jnp.sum(gp * probs, axis=-1, keepdims=True)) * SCALE
    for i, t, rows, c in dm.cells():
        query = proj[t, rows, c : c + HD].astype(BF)
        keys = proj[t, rows, half + c : half + c + HD].astype(BF)
        gs = scores[i].astype(BF)
        gproj[t, rows, c : c + HD] = nn(gs, keys)
        gproj[t, rows, half + c : half + c + HD] = tn(gs, query)
    grad_first = None
    for t in range(2):
        ct["vecs"][6:7, t * half : (t + 1) * half] = total_rows(gproj[t, :, 0:half])
        ct["vecs"][7:8, t * half : (t + 1) * half] = total_rows(gproj[t, :, 2 * half :])
        part = nt(gproj[t].astype(BF), w[t, 0 : dm.width, 0 : 3 * half])
        grad_first = part if grad_first is None else grad_first + part
    unit = st["unit_one"][...]
    gain_one, shift_one = total_rows(grad_first * unit), total_rows(grad_first)
    for i, v in enumerate((gain_one, gain_two, shift_one, shift_attn, shift_two, shift_branch)):
        ct["vecs"][i : i + 1, :] = v
    return grad_resid + norm_back(grad_first, unit, st["factors"][0], vecs[0:1, :])


def parameter_grads(dm, st, ct, grads, slots):
    half, fh = dm.half, dm.fh
    block = dm.width // dm.shards

    def keep(t, column, value):
        for f in range(dm.shards):
            rows = value[f * block : (f + 1) * block].astype(BF)
            grads[slots[t][f], :, column : column + value.shape[1]] = rows

    for t in range(2):
        keep(t, dm.o_down, tn(ct["branch"][...], st["active"][t]))
        keep(t, dm.o_up, tn(st["second"][...], ct["hidden"][t]))
        keep(t, dm.o_out, tn(ct["attn"][...], st["mixed"][t].astype(BF)))
        keep(t, 0, tn(st["first"][...], ct["proj"][t].astype(BF)))
    own_first = lax.axis_index("tensor") == 0
    plain = ct["vecs"][0:6, :]
    turned = jnp.concatenate([plain[:, half:], plain[:, 0:half]], axis=1)
    plain = jnp.where(own_first, plain, turned)
    share, up_share = half // dm.shards, fh // dm.shards
    per = fh // dm.width
    for t in range(2):
        stack = jnp.concatenate([plain, ct["vecs"][6:8, :]], axis=0)[:, t * half : (t + 1) * half]
        up = jnp.concatenate([ct["vecs"][8 + t * per + j : 9 + t * per + j, :] for j in range(per)], axis=1)
        for f in range(dm.shards):
            piece = jnp.concatenate([stack[:, f * share : (f + 1) * share], jnp.zeros((8, EXT - share), F32)], axis=1)
            up_piece = up[:, f * up_share : (f + 1) * up_share]
            up_piece = jnp.concatenate([up_piece, jnp.zeros((1, EXT - up_share), F32)], axis=1)
            piece = jnp.concatenate([piece, up_piece, jnp.zeros((block - 9, EXT), F32)], axis=0)
            grads[slots[t][f], :, dm.o_ext : dm.o_up] = piece.astype(BF)


def spread(dm, ref, get):
    pad = jnp.zeros((ROW_STEP - dm.seq, dm.width), F32)
    for m in range(2):
        ref[m * ROW_STEP : m * ROW_STEP + dm.seq, :] = get(m)
        ref[m * ROW_STEP + dm.seq : (m + 1) * ROW_STEP, :] = pad


def image(dm, value, m):
    return value[m * ROW_STEP : m * ROW_STEP + dm.seq, :]


def named(shapes, refs):
    return dict(zip(shapes, refs)), refs[len(shapes) :]


def padded_images(dm, ref, out, rows, raw, sem):
    copy = pltpu.make_async_copy(ref, raw, sem.at[0])
    copy.start()
    rows[dm.seq : 96, :] = jnp.zeros((96 - dm.seq, dm.width), F32)
    copy.wait()
    value = raw[...].astype(F32)
    for m in range(2):
        rows[0 : dm.seq, :] = value[:, m, :]
        out[m] = rows[...].astype(BF)


def kernel_tokens(dm, tokens, out, rows, raw, sem):
    padded_images(dm, tokens, out, rows, raw, sem)


def kernel_cotangents(dm, count_ref, out_grad, out, rows, raw, sem):
    live = [live_of(count_ref, m) for m in range(2)]
    out[2, 0:16, :] = jnp.concatenate(
        [jnp.full((1, dm.width), v, F32) for v in live] + [jnp.zeros((14, dm.width), F32)], axis=0
    ).astype(BF)
    padded_images(dm, out_grad, out, rows, raw, sem)


def kernel_first(dm, layout, ring, images, cotangents, *refs):
    pieces, refs = refs[:-7], refs[-7:]
    w, out, proj, probs, mixed, rows, sems = refs
    st = dict(proj=proj, probs=probs, mixed=mixed)
    block = dm.width // dm.shards
    early, late, owners = [], [], {}
    if ring:
        place = picked(RING_PLACE, lax.axis_index("fsdp"))
        sign = 1 - 2 * lax.axis_index("tensor")
    for n, (t, array, row, offset) in enumerate(layout):
        if ring:
            key = offset % dm.shards
            if key not in owners:
                there = lax.rem(place + sign * key + 2 * dm.shards, dm.shards)
                owners[key] = pl.multiple_of(picked(GRID_RING, there) * block, 16)
            where = pl.ds(owners[key], block)
        else:
            where = pl.ds(offset * block, block)
        for j, (lo, hi) in enumerate(((0, dm.o_up), (dm.o_up, dm.packed))):
            source = pieces[array].at[pl.ds(row, block), pl.ds(lo, hi - lo)]
            copy = pltpu.make_async_copy(source, w.at[t, where, pl.ds(lo, hi - lo)], sems.at[j, n])
            (early, late)[j].append(copy)
    for copy in early + late:
        copy.start()
    for m in range(2):
        w[m, dm.o_image : dm.o_grad, 0 : dm.width] = images[m]
        w[m, dm.o_grad : dm.w_rows, 0 : dm.width] = cotangents[m]
        rows[m * ROW_STEP : (m + 1) * ROW_STEP, :] = images[m].astype(F32)[0:ROW_STEP]
    for copy in early:
        copy.wait()
    extra = [
        [w[t, f * block : f * block + 16, dm.o_ext : dm.o_up].astype(F32) for f in range(dm.shards)] for t in range(2)
    ]
    share, up_share = dm.half // dm.shards, dm.fh // dm.shards
    small = [
        jnp.concatenate([v[0:8, 0:share] for v in extra[t]], axis=1) for t in range(2)
    ]
    own_first = lax.axis_index("tensor") == 0
    straight = jnp.concatenate(small, axis=1)
    turned = jnp.concatenate(small[::-1], axis=1)
    vecs = [jnp.where(own_first, straight, turned)[0:6], straight[6:8]]
    per = dm.fh // dm.width
    for t in range(2):
        up = jnp.concatenate([v[8:9, 0:up_share] for v in extra[t]], axis=1)
        vecs += [up[:, j * dm.width : (j + 1) * dm.width] for j in range(per)]
    vecs.append(cotangents[2, 0:16, :].astype(F32)[0:2])
    vecs.append(jnp.zeros((6 - 2 * per, dm.width), F32))
    vecs = jnp.concatenate(vecs, axis=0)
    w[0, dm.o_vecs : dm.o_image, 0 : dm.width] = vecs.astype(BF)
    used = lax.axis_index("section") == 0

    @pl.when(used)
    def _():
        rows[...] = forward_attention(dm, rows[...], w, vecs, st, False)

    for copy in late:
        copy.wait()

    @pl.when(used)
    def _():
        output = forward_mlp(dm, rows[...], w, vecs, st, False)
        for m in range(2):
            out[m, 0] = image(dm, output, m).astype(BF)


def vectors_of(dm, w):
    return w[0, dm.o_vecs : dm.o_image, 0 : dm.width].astype(F32)


def live_of(count_ref, m):
    return (lax.axis_index("tensor") < count_ref[0, m]).astype(F32)


def ring_slots(dm, ring):
    if not ring:
        return [range(t * dm.shards, (t + 1) * dm.shards) for t in range(2)]
    place = picked(RING_PLACE, lax.axis_index("fsdp"))
    found = [[], []]
    for p in RING_PLACE:
        ahead = jnp.where(lax.axis_index("tensor") == 0, p - place, place - p)
        ahead = lax.rem(ahead + dm.shards, dm.shards)
        found[0].append(picked(KEPT_OWN, ahead))
        found[1].append(picked(KEPT_OTHER, ahead))
    return found


def kernel_second(dm, h1, w, acts, grad_in, *refs):
    st, refs = named(dm.state_shapes(), refs)
    ct, refs = named(dm.cotangent_shapes(), refs)
    work, _ = named(dm.work_shapes(), refs)
    rows = work["rows"]
    last = lax.axis_index("section") != 0

    def take(start):
        for m in range(2):
            value = w[m, start : start + 96, 0 : dm.width].astype(F32)
            rows[m * ROW_STEP : (m + 1) * ROW_STEP, :] = value[0:ROW_STEP]

    @pl.when(jnp.logical_not(last))
    def _():
        take(dm.o_image)

    @pl.when(last)
    def _():
        spread(dm, rows, lambda m: h1[m, 0].astype(F32))

    vecs = vectors_of(dm, w)
    output = forward_mlp(dm, forward_attention(dm, rows[...], w, vecs, st, True), w, vecs, st, True)
    for m in range(2):
        acts[m, 0] = (image(dm, output, m) * vecs[12 + m : 13 + m]).astype(BF)

    @pl.when(last)
    def _():
        take(dm.o_grad)
        for m in range(2):
            rows[m * ROW_STEP : (m + 1) * ROW_STEP, :] = (
                rows[m * ROW_STEP : (m + 1) * ROW_STEP, :] * vecs[12 + m : 13 + m]
            )
        grad = layer_backward(dm, rows[...], w, vecs, st, ct, work)
        for m in range(2):
            grad_in[m, 0] = image(dm, grad, m).astype(BF)


def kernel_third(dm, ring, incoming, w, own, *refs):
    st, refs = named(dm.state_shapes(), refs)
    given, refs = named(dm.cotangent_shapes(), refs)
    grad_in, grads, *refs = refs
    ct, refs = named(dm.cotangent_shapes(), refs)
    work, _ = named(dm.work_shapes(), refs)
    rows = work["rows"]
    last = lax.axis_index("section") != 0

    @pl.when(jnp.logical_not(last))
    def _():
        spread(dm, rows, lambda m: incoming[m, 0].astype(F32))
        grad = layer_backward(dm, rows[...], w, vectors_of(dm, w), st, ct, work)
        for m in range(2):
            grad_in[m, 0] = image(dm, grad, m).astype(BF)

    @pl.when(last)
    def _():
        grad_in[...] = own[...]
        for name in ct:
            ct[name][...] = given[name][...]

    parameter_grads(dm, st, ct, grads, ring_slots(dm, ring))


def kernel_unpack(dm, *refs):
    terms, (g_qkv, g_out, g_up, g_down, g_head, g_upb, g_gain, g_shift) = refs[:-8], refs[-8:]
    half, fh = dm.half, dm.fh

    def total(rows, lo, count):
        return sum(ref[rows, lo : lo + count].astype(F32) for ref in terms)

    every = slice(None)
    for k in range(3):
        g_qkv[k] = total(every, k * half, half)
    g_out[...] = total(every, dm.o_out, half)
    g_up[...] = total(every, dm.o_up, fh)
    g_down[...] = total(every, dm.o_down, fh)
    ext = total(slice(0, 16), dm.o_ext, EXT)
    share, up_share = half // dm.shards, fh // dm.shards
    g_gain[0] = ext[0:2, 0:share]
    g_shift[0] = ext[2:6, 0:share]
    g_head[0] = ext[6:8, 0:share]
    g_upb[...] = ext[8:9, 0:up_share]


VM = pl.BlockSpec(memory_space=pltpu.VMEM)
AN = pl.BlockSpec(memory_space=pl.ANY)
SM = pl.BlockSpec(memory_space=pltpu.SMEM)


def call(kernel, ins, outs, args, scratch=(), limit=16):
    return pl.pallas_call(
        kernel,
        in_specs=ins,
        out_specs=[VM] * len(outs),
        out_shape=[jax.ShapeDtypeStruct(s, d) for s, d in outs],
        scratch_shapes=list(scratch),
        compiler_params=pltpu.CompilerParams(vmem_limit_bytes=limit * 2**20),
    )(*args)


def onward(value, cycle):
    count = len(cycle)
    route = []
    for i in range(count):
        route.append((cycle[i], cycle[(i + 1) % count]))
        route.append((count + cycle[i], count + cycle[(i - 1) % count]))
    return lax.ppermute(value, ("tensor", "fsdp"), route)


def gather_ring(block, images, cycle, swap):
    far = len(cycle) // 2
    own, other = [block], [lax.ppermute(block, "tensor", swap)]
    for step in range(far):
        own.append(onward(own[-1], cycle))
        if step + 1 < far:
            other.append(onward(other[-1], cycle))
    found, places = own + other, [(0, -s) for s in range(far + 1)] + [(1, -s) for s in range(far)]
    for t, values in ((1, own), (0, other)):
        for step in range(1, len(values)):
            value = values[step]
            if t == 1 and step < far and step % 2 == 1:
                n = step // 2
                value, ready = lax.optimization_barrier((value, images[n]))
                images = images[:n] + [ready] + images[n + 1 :]
            found.append(lax.ppermute(value, "tensor", swap))
            places.append((t, step))
    layout = [(t, i, 0, offset) for i, (t, offset) in enumerate(places)]
    return found, layout, images


def reduce_ring(blocks, outputs, cycle, swap):
    count = len(cycle)
    early = 3
    first = lax.ppermute(blocks[count : count + early], "tensor", swap)
    later = lax.ppermute(blocks[count + early :], "tensor", swap)

    def part(i, *more):
        given = first[i] if i < early else later[i - early]
        return sum(v.astype(F32) for v in (blocks[i], given) + more).astype(BF)

    def after(value, sent):
        return lax.optimization_barrier((value, sent))[0]

    own = onward(part(0), cycle)
    sent = part(1)
    other = onward(sent, cycle)
    for i in range(2, count, 2):
        sent = part(i, after(own, sent))
        own = onward(sent, cycle)
        if i + 1 < count - 1:
            sent = part(i + 1, after(other, sent))
            other = onward(sent, cycle)
    other = lax.ppermute(other, "tensor", swap)
    outputs = after(outputs, sent)
    return (blocks[count - 1], later[count - 1 - early], own, other), outputs


def per_device(tokens, out_grad, image_count, w_qkv, w_out, w_up, w_down, head_bias, up_bias, gains, shifts):
    seq, width = tokens.shape[2:]
    shards = lax.axis_size("fsdp")
    ring = shards == len(GRID_RING)
    hidden = w_up.shape[2] * 2
    dm = Dims(seq, width, hidden, len(GRID_RING))
    block = width // dm.shards
    swap = [(0, 1), (1, 0)]
    vectors = (head_bias, up_bias, gains, shifts)
    raw = [jnp.transpose(v[:, 0], (1, 0, 2)) for v in (tokens, out_grad)]
    space = [pltpu.VMEM((96, width), F32), pltpu.VMEM((seq, 2, width), BF), pltpu.SemaphoreType.DMA((1,))]
    images = [
        call(functools.partial(kernel_tokens, dm), [AN], [((2, 96, width), BF)], raw[:1], space)[0],
        call(
            functools.partial(kernel_cotangents, dm),
            [SM, AN],
            [((3, 96, width), BF)],
            (image_count.T, raw[1]),
            space,
        )[0],
    ]
    if ring:
        places = [(w_qkv[0, :, k], 0, k * dm.half) for k in range(3)]
        places += [(w_out[0].T, 0, dm.o_out), (w_up[0], 0, dm.o_up), (w_down[0].T, 0, dm.o_down)]
        places += [(v, r, dm.o_ext) for v, r in ((gains[0], 0), (shifts[0], 2), (head_bias[0], 6), (up_bias, 8))]
        packed = sum(
            jnp.pad(v, ((r, block - r - v.shape[0]), (c, dm.packed - c - v.shape[1]))) for v, r, c in places
        )
        found, layout, images = gather_ring(packed, images, GRID_RING, swap)
    else:
        rows = jnp.concatenate([w_qkv[0].reshape(w_qkv.shape[1], -1), w_out[0].T, w_up[0], w_down[0].T], axis=1)
        rows = lax.all_gather(rows, "fsdp", axis=0, tiled=True)
        front = dm.o_ext
        small = jnp.concatenate([gains[0], shifts[0], head_bias[0]], axis=0)
        small = lax.all_gather(small, "fsdp", axis=1, tiled=True)
        up = lax.all_gather(up_bias, "fsdp", axis=1, tiled=True)
        small = jnp.moveaxis(small.reshape(8, dm.shards, -1), 1, 0)
        ext = jnp.concatenate(
            [
                jnp.pad(small, ((0, 0), (0, 0), (0, EXT - small.shape[2]))),
                jnp.pad(
                    up.reshape(dm.shards, 1, -1), ((0, 0), (0, block - 9), (0, EXT - up.shape[1] // dm.shards))
                ),
            ],
            axis=1,
        )
        rows = jnp.concatenate([rows[:, :front], ext.reshape(width, EXT), rows[:, front:]], axis=1)
        found = [rows, lax.ppermute(rows, "tensor", swap)]
        layout = [(t, t, i * block, i) for t in range(2) for i in range(dm.shards)]
    states = dm.state_shapes()
    cotangents = dm.cotangent_shapes()
    shape = tokens.shape
    buffers = lambda shapes: [pltpu.VMEM(*v) for v in shapes]
    work = buffers(dm.work_shapes().values())
    w, low0 = call(
        functools.partial(kernel_first, dm, layout, ring),
        [VM, VM] + [AN] * len(found),
        [((2, dm.w_rows, dm.packed), BF), (shape, BF)],
        (*images, *found),
        scratch=buffers([states["proj"], states["probs"], states["mixed"], ((dm.rows, width), F32)])
        + [pltpu.SemaphoreType.DMA((2, len(layout)))],
    )
    h1 = lax.ppermute(low0, "section", [(0, 1)])
    kept = list(states.values()) + list(cotangents.values())
    acts, grad1, *kept = call(
        functools.partial(kernel_second, dm),
        [VM] * 2,
        [(shape, BF), (shape, BF)] + kept,
        (h1, w),
        scratch=work,
    )
    incoming = lax.ppermute(grad1, "section", [(1, 0)])
    in_grads, blocks = call(
        functools.partial(kernel_third, dm, ring),
        [VM] * (3 + len(kept)),
        [(shape, BF), ((2 * dm.shards, block, dm.packed), BF)],
        (incoming, w, grad1) + tuple(kept),
        scratch=buffers(cotangents.values()) + work,
    )
    if ring:
        terms, (acts, in_grads) = reduce_ring(blocks, (acts, in_grads), GRID_RING, swap)
        shapes = [(3, block, dm.half), (block, dm.half), (block, dm.fh), (block, dm.fh)] + [v.shape for v in vectors]
        g_qkv, g_out, g_up, g_down, *small = call(
            functools.partial(kernel_unpack, dm), [VM] * len(terms), [(v, F32) for v in shapes], terms
        )
        grads = [jnp.transpose(g_qkv, (1, 0, 2))[None], g_out.T[None], g_up[None], g_down.T[None], *small]
    else:
        half = dm.half
        mine = blocks[: dm.shards].astype(F32)
        mine += lax.ppermute(blocks[dm.shards :], "tensor", swap).astype(F32)
        mine = mine.reshape(width, dm.packed)
        body = jnp.concatenate([mine[:, : dm.o_ext], mine[:, dm.o_up :]], axis=1)
        body = lax.psum_scatter(body, "fsdp", scatter_dimension=0, tiled=True)
        up_at, down_at = dm.o_ext, dm.o_ext + dm.fh
        share, up_share = half // dm.shards, dm.fh // dm.shards
        ext = mine[:, dm.o_ext : dm.o_up].reshape(dm.shards, block, EXT)
        small = jnp.moveaxis(ext[:, 0:8, 0:share], 0, 1).reshape(8, half)
        small = lax.psum_scatter(small, "fsdp", scatter_dimension=1, tiled=True)
        up = lax.psum_scatter(ext[:, 8, 0:up_share].reshape(-1), "fsdp", scatter_dimension=0, tiled=True)
        grads = [
            body[:, : 3 * half].reshape(w_qkv.shape),
            body[:, dm.o_out : up_at].T[None],
            body[:, up_at : down_at][None],
            body[:, down_at:].T[None],
            small[6:8][None],
            up[None],
            small[0:2][None],
            small[2:6][None],
        ]
    return (acts[None], in_grads[None], *grads)


def solution(mesh):
    both = ("tensor", "fsdp")
    params = (
        P("section", "fsdp", None, "tensor"),
        P("section", "tensor", "fsdp"),
        P("section", "fsdp", "tensor"),
        P("section", "tensor", "fsdp"),
        P("section", None, both),
        P("section", both),
        P("section", None, both),
        P("section", None, both),
    )
    images = P(None, ("fsdp", "tensor"), None, None)
    layered = P("section", None, ("fsdp", "tensor"), None, None)
    return jax.shard_map(
        per_device,
        mesh=mesh,
        in_specs=(images, images, P(None, "fsdp")) + params,
        out_specs=(layered, layered) + params,
        check_vma=False,
    )
```

```python
import functools
import math

import jax
import jax.numpy as jnp
from jax import lax
from jax.experimental import pallas as pl
from jax.experimental.pallas import tpu as pltpu
from jax.sharding import PartitionSpec as P

HD = 64
EPS = 1e-06
INV_ROOT_TWO = 0.7071067811865476
INV_ROOT_TWO_PI = 0.3989422804014327
SCALE = 1.0 / math.sqrt(HD)
BF = jnp.bfloat16
F32 = jnp.float32
GRID_RING = (0, 1, 3, 5, 7, 6, 4, 2)
RING_PLACE = tuple(GRID_RING.index(i) for i in range(len(GRID_RING)))
KEPT_OWN = (7, 6, 4, 2, 0, 9, 11, 13)
KEPT_OTHER = (15, 5, 3, 1, 8, 10, 12, 14)
ROW_STEP = 88
EXT = 128


def dot(a, b, dims):
    return lax.dot_general(a, b, (dims, ((), ())), preferred_element_type=F32)


def nn(a, b):
    return dot(a, b, ((1,), (0,)))


def nt(a, b):
    return dot(a, b, ((1,), (1,)))


def tn(a, b):
    return dot(a, b, ((0,), (0,)))


def norm(value):
    mean = jnp.mean(value, axis=-1, keepdims=True)
    centred = value - mean
    var = jnp.mean(centred * centred, axis=-1, keepdims=True)
    factor = lax.rsqrt(var + EPS)
    return centred * factor, factor


def norm_back(grad, unit, factor, gain):
    scaled = grad * gain
    plain = jnp.mean(scaled, axis=-1, keepdims=True)
    along = jnp.mean(scaled * unit, axis=-1, keepdims=True)
    return (scaled - plain - unit * along) * factor


def picked(options, index):
    value = jnp.int32(options[0])
    for i in range(1, len(options)):
        value = jnp.where(index == i, jnp.int32(options[i]), value)
    return value


class Dims:
    def __init__(self, seq, width, hidden, shards):
        self.seq, self.width, self.hidden, self.shards = seq, width, hidden, shards
        self.half = width // 2
        self.fh = hidden // 2
        self.heads = self.half // HD
        self.o_out = 3 * self.half
        self.o_ext = self.o_out + self.half
        self.o_up = self.o_ext + EXT
        self.o_down = self.o_up + self.fh
        self.packed = self.o_down + self.fh
        self.rows = 2 * ROW_STEP
        self.o_vecs = width
        self.o_image = width + 16
        self.o_grad = self.o_image + 96
        self.w_rows = self.o_grad + 96

    def state_shapes(self):
        r, w = self.rows, self.width
        return dict(
            proj=((2, r, 3 * self.half), F32),
            probs=((4 * self.heads, ROW_STEP, ROW_STEP), F32),
            mixed=((2, r, self.half), F32),
            unit_one=((r, w), F32),
            factors=((2, r, 1), F32),
            first=((r, w), BF),
            unit_two=((r, w), F32),
            second=((r, w), BF),
            slope=((2, r, self.fh), F32),
            active=((2, r, self.fh), BF),
        )

    def cotangent_shapes(self):
        r, w = self.rows, self.width
        return dict(
            branch=((r, w), BF),
            hidden=((2, r, self.fh), BF),
            attn=((r, w), BF),
            proj=((2, r, 3 * self.half), F32),
            vecs=((16, w), F32),
        )

    def work_shapes(self):
        return dict(
            rows=((self.rows, self.width), F32),
            mixed=((2, self.rows, self.half), F32),
            scores=((4 * self.heads, ROW_STEP, ROW_STEP), F32),
        )

    def cells(self):
        for t in range(2):
            for m in range(2):
                for h in range(self.heads):
                    rows = slice(m * ROW_STEP, (m + 1) * ROW_STEP)
                    yield (t * 2 + m) * self.heads + h, t, rows, h * HD


def forward_attention(dm, state, w, vecs, st, keep):
    half = dm.half
    unit, factor = norm(state)
    first = (unit * vecs[0:1, :] + vecs[2:3, :]).astype(BF)
    if keep:
        st["unit_one"][...] = unit
        st["factors"][0] = factor
        st["first"][...] = first
    proj, mixed = st["proj"], st["mixed"]
    for t in range(2):
        value = nn(first, w[t, 0 : dm.width, 0 : 3 * half])
        proj[t, :, 0:half] = value[:, 0:half] + vecs[6:7, t * half : (t + 1) * half]
        proj[t, :, half : 2 * half] = value[:, half : 2 * half]
        proj[t, :, 2 * half :] = value[:, 2 * half :] + vecs[7:8, t * half : (t + 1) * half]
    for i, t, rows, c in dm.cells():
        query, keys = proj[t, rows, c : c + HD], proj[t, rows, half + c : half + c + HD]
        st["probs"][i] = nt(query.astype(BF), keys.astype(BF))
    scores = st["probs"][...] * SCALE
    column = lax.broadcasted_iota(jnp.int32, scores.shape, 2)
    scores = jnp.where(column < dm.seq, scores, -1e30)
    expo = jnp.exp(scores - jnp.max(scores, axis=-1, keepdims=True))
    st["probs"][...] = expo * (1.0 / jnp.sum(expo, axis=-1, keepdims=True))
    for i, t, rows, c in dm.cells():
        values = proj[t, rows, 2 * half + c : 2 * half + c + HD]
        mixed[t, rows, c : c + HD] = nn(st["probs"][i].astype(BF), values.astype(BF))
    resid = state + vecs[3:4, :]
    for t in range(2):
        resid += nt(mixed[t].astype(BF), w[t, 0 : dm.width, dm.o_out : dm.o_out + half])
    return resid


def forward_mlp(dm, resid, w, vecs, st, keep):
    fh = dm.fh
    unit, factor = norm(resid)
    second = (unit * vecs[1:2, :] + vecs[4:5, :]).astype(BF)
    if keep:
        st["unit_two"][...] = unit
        st["factors"][1] = factor
        st["second"][...] = second
    output = resid + vecs[5:6, :]
    per = fh // dm.width
    for t in range(2):
        bias = jnp.concatenate([vecs[8 + t * per + j : 9 + t * per + j, :] for j in range(per)], axis=1)
        hidden = nn(second, w[t, 0 : dm.width, dm.o_up : dm.o_up + fh]) + bias
        curve = 0.5 * (1.0 + lax.erf(hidden * INV_ROOT_TWO))
        active = (hidden * curve).astype(BF)
        if keep:
            st["slope"][t] = curve + hidden * jnp.exp(-0.5 * hidden * hidden) * INV_ROOT_TWO_PI
            st["active"][t] = active
        output += nt(active, w[t, 0 : dm.width, dm.o_down : dm.o_down + fh])
    return output


def total_rows(value):
    return jnp.sum(value, axis=0, keepdims=True)


def layer_backward(dm, grad, w, vecs, st, ct, work):
    half, fh = dm.half, dm.fh
    low = grad.astype(BF)
    ct["branch"][...] = low
    shift_branch = total_rows(low.astype(F32))
    per = fh // dm.width
    grad_second = None
    for t in range(2):
        raw = nn(low, w[t, 0 : dm.width, dm.o_down : dm.o_down + fh]) * st["slope"][t]
        up_bias = total_rows(raw)
        for j in range(per):
            ct["vecs"][8 + t * per + j : 9 + t * per + j, :] = up_bias[:, j * dm.width : (j + 1) * dm.width]
        grad_hidden = raw.astype(BF)
        ct["hidden"][t] = grad_hidden
        part = nt(grad_hidden, w[t, 0 : dm.width, dm.o_up : dm.o_up + fh])
        grad_second = part if grad_second is None else grad_second + part
    unit = st["unit_two"][...]
    gain_two, shift_two = total_rows(grad_second * unit), total_rows(grad_second)
    grad_resid = grad + norm_back(grad_second, unit, st["factors"][1], vecs[1:2, :])
    low = grad_resid.astype(BF)
    ct["attn"][...] = low
    shift_attn = total_rows(low.astype(F32))
    proj, gproj, gmix, scores = st["proj"], ct["proj"], work["mixed"], work["scores"]
    for t in range(2):
        gmix[t] = nn(low, w[t, 0 : dm.width, dm.o_out : dm.o_out + half])
    for i, t, rows, c in dm.cells():
        values = proj[t, rows, 2 * half + c : 2 * half + c + HD].astype(BF)
        gm = gmix[t, rows, c : c + HD].astype(BF)
        scores[i] = nt(gm, values)
        gproj[t, rows, 2 * half + c : 2 * half + c + HD] = tn(st["probs"][i].astype(BF), gm)
    probs, gp = st["probs"][...], scores[...]
    scores[...] = probs * (gp - jnp.sum(gp * probs, axis=-1, keepdims=True)) * SCALE
    for i, t, rows, c in dm.cells():
        query = proj[t, rows, c : c + HD].astype(BF)
        keys = proj[t, rows, half + c : half + c + HD].astype(BF)
        gs = scores[i].astype(BF)
        gproj[t, rows, c : c + HD] = nn(gs, keys)
        gproj[t, rows, half + c : half + c + HD] = tn(gs, query)
    grad_first = None
    for t in range(2):
        ct["vecs"][6:7, t * half : (t + 1) * half] = total_rows(gproj[t, :, 0:half])
        ct["vecs"][7:8, t * half : (t + 1) * half] = total_rows(gproj[t, :, 2 * half :])
        part = nt(gproj[t].astype(BF), w[t, 0 : dm.width, 0 : 3 * half])
        grad_first = part if grad_first is None else grad_first + part
    unit = st["unit_one"][...]
    gain_one, shift_one = total_rows(grad_first * unit), total_rows(grad_first)
    for i, v in enumerate((gain_one, gain_two, shift_one, shift_attn, shift_two, shift_branch)):
        ct["vecs"][i : i + 1, :] = v
    return grad_resid + norm_back(grad_first, unit, st["factors"][0], vecs[0:1, :])


def parameter_grads(dm, st, ct, grads, slots):
    half, fh = dm.half, dm.fh
    block = dm.width // dm.shards

    def keep(t, column, value):
        for f in range(dm.shards):
            rows = value[f * block : (f + 1) * block].astype(BF)
            grads[slots[t][f], :, column : column + value.shape[1]] = rows

    for t in range(2):
        keep(t, dm.o_down, tn(ct["branch"][...], st["active"][t]))
        keep(t, dm.o_up, tn(st["second"][...], ct["hidden"][t]))
        keep(t, dm.o_out, tn(ct["attn"][...], st["mixed"][t].astype(BF)))
        keep(t, 0, tn(st["first"][...], ct["proj"][t].astype(BF)))
    own_first = lax.axis_index("tensor") == 0
    plain = ct["vecs"][0:6, :]
    turned = jnp.concatenate([plain[:, half:], plain[:, 0:half]], axis=1)
    plain = jnp.where(own_first, plain, turned)
    share, up_share = half // dm.shards, fh // dm.shards
    per = fh // dm.width
    for t in range(2):
        stack = jnp.concatenate([plain, ct["vecs"][6:8, :]], axis=0)[:, t * half : (t + 1) * half]
        up = jnp.concatenate([ct["vecs"][8 + t * per + j : 9 + t * per + j, :] for j in range(per)], axis=1)
        for f in range(dm.shards):
            piece = jnp.concatenate([stack[:, f * share : (f + 1) * share], jnp.zeros((8, EXT - share), F32)], axis=1)
            up_piece = up[:, f * up_share : (f + 1) * up_share]
            up_piece = jnp.concatenate([up_piece, jnp.zeros((1, EXT - up_share), F32)], axis=1)
            piece = jnp.concatenate([piece, up_piece, jnp.zeros((block - 9, EXT), F32)], axis=0)
            grads[slots[t][f], :, dm.o_ext : dm.o_up] = piece.astype(BF)


def spread(dm, ref, get):
    pad = jnp.zeros((ROW_STEP - dm.seq, dm.width), F32)
    for m in range(2):
        ref[m * ROW_STEP : m * ROW_STEP + dm.seq, :] = get(m)
        ref[m * ROW_STEP + dm.seq : (m + 1) * ROW_STEP, :] = pad


def image(dm, value, m):
    return value[m * ROW_STEP : m * ROW_STEP + dm.seq, :]


def named(shapes, refs):
    return dict(zip(shapes, refs)), refs[len(shapes) :]


def padded_images(dm, ref, out, rows, raw, sem):
    copy = pltpu.make_async_copy(ref, raw, sem.at[0])
    copy.start()
    rows[dm.seq : 96, :] = jnp.zeros((96 - dm.seq, dm.width), F32)
    copy.wait()
    value = raw[...].astype(F32)
    for m in range(2):
        rows[0 : dm.seq, :] = value[:, m, :]
        out[m] = rows[...].astype(BF)


def kernel_tokens(dm, tokens, out, rows, raw, sem):
    padded_images(dm, tokens, out, rows, raw, sem)


def kernel_cotangents(dm, count_ref, out_grad, out, rows, raw, sem):
    live = [live_of(count_ref, m) for m in range(2)]
    out[2, 0:16, :] = jnp.concatenate(
        [jnp.full((1, dm.width), v, F32) for v in live] + [jnp.zeros((14, dm.width), F32)], axis=0
    ).astype(BF)
    padded_images(dm, out_grad, out, rows, raw, sem)


def kernel_first(dm, layout, ring, images, cotangents, *refs):
    pieces, refs = refs[:-7], refs[-7:]
    w, out, proj, probs, mixed, rows, sems = refs
    st = dict(proj=proj, probs=probs, mixed=mixed)
    block = dm.width // dm.shards
    early, late, owners = [], [], {}
    if ring:
        place = picked(RING_PLACE, lax.axis_index("fsdp"))
        sign = 1 - 2 * lax.axis_index("tensor")
    for n, (t, array, row, offset) in enumerate(layout):
        if ring:
            key = offset % dm.shards
            if key not in owners:
                there = lax.rem(place + sign * key + 2 * dm.shards, dm.shards)
                owners[key] = pl.multiple_of(picked(GRID_RING, there) * block, 16)
            where = pl.ds(owners[key], block)
        else:
            where = pl.ds(offset * block, block)
        for j, (lo, hi) in enumerate(((0, dm.o_up), (dm.o_up, dm.packed))):
            source = pieces[array].at[pl.ds(row, block), pl.ds(lo, hi - lo)]
            copy = pltpu.make_async_copy(source, w.at[t, where, pl.ds(lo, hi - lo)], sems.at[j, n])
            (early, late)[j].append(copy)
    for copy in early + late:
        copy.start()
    for m in range(2):
        w[m, dm.o_image : dm.o_grad, 0 : dm.width] = images[m]
        w[m, dm.o_grad : dm.w_rows, 0 : dm.width] = cotangents[m]
        rows[m * ROW_STEP : (m + 1) * ROW_STEP, :] = images[m].astype(F32)[0:ROW_STEP]
    for copy in early:
        copy.wait()
    extra = [
        [w[t, f * block : f * block + 16, dm.o_ext : dm.o_up].astype(F32) for f in range(dm.shards)] for t in range(2)
    ]
    share, up_share = dm.half // dm.shards, dm.fh // dm.shards
    small = [
        jnp.concatenate([v[0:8, 0:share] for v in extra[t]], axis=1) for t in range(2)
    ]
    own_first = lax.axis_index("tensor") == 0
    straight = jnp.concatenate(small, axis=1)
    turned = jnp.concatenate(small[::-1], axis=1)
    vecs = [jnp.where(own_first, straight, turned)[0:6], straight[6:8]]
    per = dm.fh // dm.width
    for t in range(2):
        up = jnp.concatenate([v[8:9, 0:up_share] for v in extra[t]], axis=1)
        vecs += [up[:, j * dm.width : (j + 1) * dm.width] for j in range(per)]
    vecs.append(cotangents[2, 0:16, :].astype(F32)[0:2])
    vecs.append(jnp.zeros((6 - 2 * per, dm.width), F32))
    vecs = jnp.concatenate(vecs, axis=0)
    w[0, dm.o_vecs : dm.o_image, 0 : dm.width] = vecs.astype(BF)
    used = lax.axis_index("section") == 0

    @pl.when(used)
    def _():
        rows[...] = forward_attention(dm, rows[...], w, vecs, st, False)

    for copy in late:
        copy.wait()

    @pl.when(used)
    def _():
        output = forward_mlp(dm, rows[...], w, vecs, st, False)
        for m in range(2):
            out[m, 0] = image(dm, output, m).astype(BF)


def vectors_of(dm, w):
    return w[0, dm.o_vecs : dm.o_image, 0 : dm.width].astype(F32)


def live_of(count_ref, m):
    return (lax.axis_index("tensor") < count_ref[0, m]).astype(F32)


def ring_slots(dm, ring):
    if not ring:
        return [range(t * dm.shards, (t + 1) * dm.shards) for t in range(2)]
    place = picked(RING_PLACE, lax.axis_index("fsdp"))
    found = [[], []]
    for p in RING_PLACE:
        ahead = jnp.where(lax.axis_index("tensor") == 0, p - place, place - p)
        ahead = lax.rem(ahead + dm.shards, dm.shards)
        found[0].append(picked(KEPT_OWN, ahead))
        found[1].append(picked(KEPT_OTHER, ahead))
    return found


def kernel_second(dm, h1, w, acts, grad_in, *refs):
    st, refs = named(dm.state_shapes(), refs)
    ct, refs = named(dm.cotangent_shapes(), refs)
    work, _ = named(dm.work_shapes(), refs)
    rows = work["rows"]
    last = lax.axis_index("section") != 0

    def take(start):
        for m in range(2):
            value = w[m, start : start + 96, 0 : dm.width].astype(F32)
            rows[m * ROW_STEP : (m + 1) * ROW_STEP, :] = value[0:ROW_STEP]

    @pl.when(jnp.logical_not(last))
    def _():
        take(dm.o_image)

    @pl.when(last)
    def _():
        spread(dm, rows, lambda m: h1[m, 0].astype(F32))

    vecs = vectors_of(dm, w)
    output = forward_mlp(dm, forward_attention(dm, rows[...], w, vecs, st, True), w, vecs, st, True)
    for m in range(2):
        acts[m, 0] = (image(dm, output, m) * vecs[12 + m : 13 + m]).astype(BF)

    @pl.when(last)
    def _():
        take(dm.o_grad)
        for m in range(2):
            rows[m * ROW_STEP : (m + 1) * ROW_STEP, :] = (
                rows[m * ROW_STEP : (m + 1) * ROW_STEP, :] * vecs[12 + m : 13 + m]
            )
        grad = layer_backward(dm, rows[...], w, vecs, st, ct, work)
        for m in range(2):
            grad_in[m, 0] = image(dm, grad, m).astype(BF)


def kernel_third(dm, ring, incoming, w, own, *refs):
    st, refs = named(dm.state_shapes(), refs)
    given, refs = named(dm.cotangent_shapes(), refs)
    grad_in, grads, *refs = refs
    ct, refs = named(dm.cotangent_shapes(), refs)
    work, _ = named(dm.work_shapes(), refs)
    rows = work["rows"]
    last = lax.axis_index("section") != 0

    @pl.when(jnp.logical_not(last))
    def _():
        spread(dm, rows, lambda m: incoming[m, 0].astype(F32))
        grad = layer_backward(dm, rows[...], w, vectors_of(dm, w), st, ct, work)
        for m in range(2):
            grad_in[m, 0] = image(dm, grad, m).astype(BF)

    @pl.when(last)
    def _():
        grad_in[...] = own[...]
        for name in ct:
            ct[name][...] = given[name][...]

    parameter_grads(dm, st, ct, grads, ring_slots(dm, ring))


def kernel_unpack(dm, *refs):
    terms, (g_qkv, g_out, g_up, g_down, g_head, g_upb, g_gain, g_shift) = refs[:-8], refs[-8:]
    half, fh = dm.half, dm.fh

    def total(rows, lo, count):
        return sum(ref[rows, lo : lo + count].astype(F32) for ref in terms)

    every = slice(None)
    for k in range(3):
        g_qkv[k] = total(every, k * half, half)
    g_out[...] = total(every, dm.o_out, half)
    g_up[...] = total(every, dm.o_up, fh)
    g_down[...] = total(every, dm.o_down, fh)
    ext = total(slice(0, 16), dm.o_ext, EXT)
    share, up_share = half // dm.shards, fh // dm.shards
    g_gain[0] = ext[0:2, 0:share]
    g_shift[0] = ext[2:6, 0:share]
    g_head[0] = ext[6:8, 0:share]
    g_upb[...] = ext[8:9, 0:up_share]


VM = pl.BlockSpec(memory_space=pltpu.VMEM)
AN = pl.BlockSpec(memory_space=pl.ANY)
SM = pl.BlockSpec(memory_space=pltpu.SMEM)


def call(kernel, ins, outs, args, scratch=(), limit=16):
    return pl.pallas_call(
        kernel,
        in_specs=ins,
        out_specs=[VM] * len(outs),
        out_shape=[jax.ShapeDtypeStruct(s, d) for s, d in outs],
        scratch_shapes=list(scratch),
        compiler_params=pltpu.CompilerParams(vmem_limit_bytes=limit * 2**20),
    )(*args)


def onward(value, cycle):
    count = len(cycle)
    route = []
    for i in range(count):
        route.append((cycle[i], cycle[(i + 1) % count]))
        route.append((count + cycle[i], count + cycle[(i - 1) % count]))
    return lax.ppermute(value, ("tensor", "fsdp"), route)


def gather_ring(block, images, cycle, swap):
    far = len(cycle) // 2
    own, other = [block], [lax.ppermute(block, "tensor", swap)]
    for step in range(far):
        own.append(onward(own[-1], cycle))
        if step + 1 < far:
            other.append(onward(other[-1], cycle))
    found, places = own + other, [(0, -s) for s in range(far + 1)] + [(1, -s) for s in range(far)]
    for t, values in ((1, own), (0, other)):
        for step in range(1, len(values)):
            value = values[step]
            if t == 1 and step < far and step % 2 == 1:
                n = step // 2
                value, ready = lax.optimization_barrier((value, images[n]))
                images = images[:n] + [ready] + images[n + 1 :]
            found.append(lax.ppermute(value, "tensor", swap))
            places.append((t, step))
    layout = [(t, i, 0, offset) for i, (t, offset) in enumerate(places)]
    return found, layout, images


def reduce_ring(blocks, outputs, cycle, swap):
    count = len(cycle)
    early = 2
    first = lax.ppermute(blocks[count : count + early], "tensor", swap)

    def part(i, *more):
        given = first[i] if i < early else later[i - early]
        return sum(v.astype(F32) for v in (blocks[i], given) + more).astype(BF)

    def after(value, sent):
        return lax.optimization_barrier((value, sent))[0]

    sent = part(0)
    own = onward(sent, cycle)
    later = lax.ppermute(after(blocks[count + early :], sent), "tensor", swap)
    sent = part(1)
    other = onward(sent, cycle)
    for i in range(2, count, 2):
        sent = part(i, after(own, sent))
        own = onward(sent, cycle)
        if i + 1 < count - 1:
            sent = part(i + 1, after(other, sent))
            other = onward(sent, cycle)
    other = lax.ppermute(other, "tensor", swap)
    outputs = after(outputs, sent)
    return (blocks[count - 1], later[count - 1 - early], own, other), outputs


def per_device(tokens, out_grad, image_count, w_qkv, w_out, w_up, w_down, head_bias, up_bias, gains, shifts):
    seq, width = tokens.shape[2:]
    shards = lax.axis_size("fsdp")
    ring = shards == len(GRID_RING)
    hidden = w_up.shape[2] * 2
    dm = Dims(seq, width, hidden, len(GRID_RING))
    block = width // dm.shards
    swap = [(0, 1), (1, 0)]
    vectors = (head_bias, up_bias, gains, shifts)
    raw = [jnp.transpose(v[:, 0], (1, 0, 2)) for v in (tokens, out_grad)]
    space = [pltpu.VMEM((96, width), F32), pltpu.VMEM((seq, 2, width), BF), pltpu.SemaphoreType.DMA((1,))]
    images = [
        call(functools.partial(kernel_tokens, dm), [AN], [((2, 96, width), BF)], raw[:1], space)[0],
        call(
            functools.partial(kernel_cotangents, dm),
            [SM, AN],
            [((3, 96, width), BF)],
            (image_count.T, raw[1]),
            space,
        )[0],
    ]
    if ring:
        places = [(w_qkv[0, :, k], 0, k * dm.half) for k in range(3)]
        places += [(w_out[0].T, 0, dm.o_out), (w_up[0], 0, dm.o_up), (w_down[0].T, 0, dm.o_down)]
        places += [(v, r, dm.o_ext) for v, r in ((gains[0], 0), (shifts[0], 2), (head_bias[0], 6), (up_bias, 8))]
        packed = sum(
            jnp.pad(v, ((r, block - r - v.shape[0]), (c, dm.packed - c - v.shape[1]))) for v, r, c in places
        )
        found, layout, images = gather_ring(packed, images, GRID_RING, swap)
    else:
        rows = jnp.concatenate([w_qkv[0].reshape(w_qkv.shape[1], -1), w_out[0].T, w_up[0], w_down[0].T], axis=1)
        rows = lax.all_gather(rows, "fsdp", axis=0, tiled=True)
        front = dm.o_ext
        small = jnp.concatenate([gains[0], shifts[0], head_bias[0]], axis=0)
        small = lax.all_gather(small, "fsdp", axis=1, tiled=True)
        up = lax.all_gather(up_bias, "fsdp", axis=1, tiled=True)
        small = jnp.moveaxis(small.reshape(8, dm.shards, -1), 1, 0)
        ext = jnp.concatenate(
            [
                jnp.pad(small, ((0, 0), (0, 0), (0, EXT - small.shape[2]))),
                jnp.pad(
                    up.reshape(dm.shards, 1, -1), ((0, 0), (0, block - 9), (0, EXT - up.shape[1] // dm.shards))
                ),
            ],
            axis=1,
        )
        rows = jnp.concatenate([rows[:, :front], ext.reshape(width, EXT), rows[:, front:]], axis=1)
        found = [rows, lax.ppermute(rows, "tensor", swap)]
        layout = [(t, t, i * block, i) for t in range(2) for i in range(dm.shards)]
    states = dm.state_shapes()
    cotangents = dm.cotangent_shapes()
    shape = tokens.shape
    buffers = lambda shapes: [pltpu.VMEM(*v) for v in shapes]
    work = buffers(dm.work_shapes().values())
    w, low0 = call(
        functools.partial(kernel_first, dm, layout, ring),
        [VM, VM] + [AN] * len(found),
        [((2, dm.w_rows, dm.packed), BF), (shape, BF)],
        (*images, *found),
        scratch=buffers([states["proj"], states["probs"], states["mixed"], ((dm.rows, width), F32)])
        + [pltpu.SemaphoreType.DMA((2, len(layout)))],
    )
    h1 = lax.ppermute(low0, "section", [(0, 1)])
    kept = list(states.values()) + list(cotangents.values())
    acts, grad1, *kept = call(
        functools.partial(kernel_second, dm),
        [VM] * 2,
        [(shape, BF), (shape, BF)] + kept,
        (h1, w),
        scratch=work,
    )
    incoming = lax.ppermute(grad1, "section", [(1, 0)])
    in_grads, blocks = call(
        functools.partial(kernel_third, dm, ring),
        [VM] * (3 + len(kept)),
        [(shape, BF), ((2 * dm.shards, block, dm.packed), BF)],
        (incoming, w, grad1) + tuple(kept),
        scratch=buffers(cotangents.values()) + work,
    )
    if ring:
        terms, (acts, in_grads) = reduce_ring(blocks, (acts, in_grads), GRID_RING, swap)
        shapes = [(3, block, dm.half), (block, dm.half), (block, dm.fh), (block, dm.fh)] + [v.shape for v in vectors]
        g_qkv, g_out, g_up, g_down, *small = call(
            functools.partial(kernel_unpack, dm), [VM] * len(terms), [(v, F32) for v in shapes], terms
        )
        grads = [jnp.transpose(g_qkv, (1, 0, 2))[None], g_out.T[None], g_up[None], g_down.T[None], *small]
    else:
        half = dm.half
        mine = blocks[: dm.shards].astype(F32)
        mine += lax.ppermute(blocks[dm.shards :], "tensor", swap).astype(F32)
        mine = mine.reshape(width, dm.packed)
        body = jnp.concatenate([mine[:, : dm.o_ext], mine[:, dm.o_up :]], axis=1)
        body = lax.psum_scatter(body, "fsdp", scatter_dimension=0, tiled=True)
        up_at, down_at = dm.o_ext, dm.o_ext + dm.fh
        share, up_share = half // dm.shards, dm.fh // dm.shards
        ext = mine[:, dm.o_ext : dm.o_up].reshape(dm.shards, block, EXT)
        small = jnp.moveaxis(ext[:, 0:8, 0:share], 0, 1).reshape(8, half)
        small = lax.psum_scatter(small, "fsdp", scatter_dimension=1, tiled=True)
        up = lax.psum_scatter(ext[:, 8, 0:up_share].reshape(-1), "fsdp", scatter_dimension=0, tiled=True)
        grads = [
            body[:, : 3 * half].reshape(w_qkv.shape),
            body[:, dm.o_out : up_at].T[None],
            body[:, up_at : down_at][None],
            body[:, down_at:].T[None],
            small[6:8][None],
            up[None],
            small[0:2][None],
            small[2:6][None],
        ]
    return (acts[None], in_grads[None], *grads)


def solution(mesh):
    both = ("tensor", "fsdp")
    params = (
        P("section", "fsdp", None, "tensor"),
        P("section", "tensor", "fsdp"),
        P("section", "fsdp", "tensor"),
        P("section", "tensor", "fsdp"),
        P("section", None, both),
        P("section", both),
        P("section", None, both),
        P("section", None, both),
    )
    images = P(None, ("fsdp", "tensor"), None, None)
    layered = P("section", None, ("fsdp", "tensor"), None, None)
    return jax.shard_map(
        per_device,
        mesh=mesh,
        in_specs=(images, images, P(None, "fsdp")) + params,
        out_specs=(layered, layered) + params,
        check_vma=False,
    )
```

```python
import functools
import math

import jax
import jax.numpy as jnp
from jax import lax
from jax.experimental import pallas as pl
from jax.experimental.pallas import tpu as pltpu
from jax.sharding import PartitionSpec as P

HD = 64
EPS = 1e-06
INV_ROOT_TWO = 0.7071067811865476
INV_ROOT_TWO_PI = 0.3989422804014327
SCALE = 1.0 / math.sqrt(HD)
BF = jnp.bfloat16
F32 = jnp.float32
GRID_RING = (0, 1, 3, 5, 7, 6, 4, 2)
RING_PLACE = tuple(GRID_RING.index(i) for i in range(len(GRID_RING)))
KEPT_OWN = (7, 6, 4, 2, 0, 9, 11, 13)
KEPT_OTHER = (15, 5, 3, 1, 8, 10, 12, 14)
ROW_STEP = 88
EXT = 128


def dot(a, b, dims):
    return lax.dot_general(a, b, (dims, ((), ())), preferred_element_type=F32)


def nn(a, b):
    return dot(a, b, ((1,), (0,)))


def nt(a, b):
    return dot(a, b, ((1,), (1,)))


def tn(a, b):
    return dot(a, b, ((0,), (0,)))


def norm(value):
    mean = jnp.mean(value, axis=-1, keepdims=True)
    centred = value - mean
    var = jnp.mean(centred * centred, axis=-1, keepdims=True)
    factor = lax.rsqrt(var + EPS)
    return centred * factor, factor


def norm_back(grad, unit, factor, gain):
    scaled = grad * gain
    plain = jnp.mean(scaled, axis=-1, keepdims=True)
    along = jnp.mean(scaled * unit, axis=-1, keepdims=True)
    return (scaled - plain - unit * along) * factor


def picked(options, index):
    value = jnp.int32(options[0])
    for i in range(1, len(options)):
        value = jnp.where(index == i, jnp.int32(options[i]), value)
    return value


class Dims:
    def __init__(self, seq, width, hidden, shards):
        self.seq, self.width, self.hidden, self.shards = seq, width, hidden, shards
        self.half = width // 2
        self.fh = hidden // 2
        self.heads = self.half // HD
        self.o_out = 3 * self.half
        self.o_ext = self.o_out + self.half
        self.o_up = self.o_ext + EXT
        self.o_down = self.o_up + self.fh
        self.packed = self.o_down + self.fh
        self.w_up = 2 * self.o_up
        self.w_down = self.w_up + hidden
        self.rows = 2 * ROW_STEP
        self.o_vecs = width
        self.o_image = width + 16
        self.o_grad = self.o_image + 96
        self.w_rows = self.o_grad + 96

    def state_shapes(self):
        r, w = self.rows, self.width
        return dict(
            proj=((2, r, 3 * self.half), F32),
            probs=((4 * self.heads, ROW_STEP, ROW_STEP), F32),
            mixed=((2, r, self.half), F32),
            unit_one=((r, w), F32),
            factors=((2, r, 1), F32),
            first=((r, w), BF),
            unit_two=((r, w), F32),
            second=((r, w), BF),
            slope=((r, 2 * self.fh), F32),
            active=((r, 2 * self.fh), BF),
        )

    def cotangent_shapes(self):
        r, w = self.rows, self.width
        return dict(
            branch=((r, w), BF),
            hidden=((r, 2 * self.fh), BF),
            attn=((r, w), BF),
            proj=((2, r, 3 * self.half), F32),
            vecs=((16, w), F32),
        )

    def work_shapes(self):
        return dict(
            rows=((self.rows, self.width), F32),
            mixed=((2, self.rows, self.half), F32),
            scores=((4 * self.heads, ROW_STEP, ROW_STEP), F32),
        )

    def cells(self):
        for t in range(2):
            for m in range(2):
                for h in range(self.heads):
                    rows = slice(m * ROW_STEP, (m + 1) * ROW_STEP)
                    yield (t * 2 + m) * self.heads + h, t, rows, h * HD


def forward_attention(dm, state, w, vecs, st, keep):
    half = dm.half
    unit, factor = norm(state)
    first = (unit * vecs[0:1, :] + vecs[2:3, :]).astype(BF)
    if keep:
        st["unit_one"][...] = unit
        st["factors"][0] = factor
        st["first"][...] = first
    proj, mixed = st["proj"], st["mixed"]
    for t in range(2):
        value = nn(first, w[0 : dm.width, t * dm.o_up : t * dm.o_up + 3 * half])
        proj[t, :, 0:half] = value[:, 0:half] + vecs[6:7, t * half : (t + 1) * half]
        proj[t, :, half : 2 * half] = value[:, half : 2 * half]
        proj[t, :, 2 * half :] = value[:, 2 * half :] + vecs[7:8, t * half : (t + 1) * half]
    for i, t, rows, c in dm.cells():
        query, keys = proj[t, rows, c : c + HD], proj[t, rows, half + c : half + c + HD]
        st["probs"][i] = nt(query.astype(BF), keys.astype(BF))
    scores = st["probs"][...] * SCALE
    column = lax.broadcasted_iota(jnp.int32, scores.shape, 2)
    scores = jnp.where(column < dm.seq, scores, -1e30)
    expo = jnp.exp(scores - jnp.max(scores, axis=-1, keepdims=True))
    st["probs"][...] = expo * (1.0 / jnp.sum(expo, axis=-1, keepdims=True))
    for i, t, rows, c in dm.cells():
        values = proj[t, rows, 2 * half + c : 2 * half + c + HD]
        mixed[t, rows, c : c + HD] = nn(st["probs"][i].astype(BF), values.astype(BF))
    resid = state + vecs[3:4, :]
    for t in range(2):
        resid += nt(mixed[t].astype(BF), w[0 : dm.width, t * dm.o_up + dm.o_out : t * dm.o_up + dm.o_ext])
    return resid


def forward_mlp(dm, resid, w, vecs, st, keep):
    fh = dm.fh
    unit, factor = norm(resid)
    second = (unit * vecs[1:2, :] + vecs[4:5, :]).astype(BF)
    if keep:
        st["unit_two"][...] = unit
        st["factors"][1] = factor
        st["second"][...] = second
    output = resid + vecs[5:6, :]
    bias = jnp.concatenate([vecs[8 + j : 9 + j, :] for j in range(2 * fh // dm.width)], axis=1)
    hidden = nn(second, w[0 : dm.width, dm.w_up : dm.w_down]) + bias
    curve = 0.5 * (1.0 + lax.erf(hidden * INV_ROOT_TWO))
    active = (hidden * curve).astype(BF)
    if keep:
        st["slope"][...] = curve + hidden * jnp.exp(-0.5 * hidden * hidden) * INV_ROOT_TWO_PI
        st["active"][...] = active
    return output + nt(active, w[0 : dm.width, dm.w_down :])


def total_rows(value):
    return jnp.sum(value, axis=0, keepdims=True)


def layer_backward(dm, grad, w, vecs, st, ct, work):
    half, fh = dm.half, dm.fh
    low = grad.astype(BF)
    ct["branch"][...] = low
    shift_branch = total_rows(low.astype(F32))
    raw = nn(low, w[0 : dm.width, dm.w_down :]) * st["slope"][...]
    up_bias = total_rows(raw)
    for j in range(2 * fh // dm.width):
        ct["vecs"][8 + j : 9 + j, :] = up_bias[:, j * dm.width : (j + 1) * dm.width]
    grad_hidden = raw.astype(BF)
    ct["hidden"][...] = grad_hidden
    grad_second = nt(grad_hidden, w[0 : dm.width, dm.w_up : dm.w_down])
    unit = st["unit_two"][...]
    gain_two, shift_two = total_rows(grad_second * unit), total_rows(grad_second)
    grad_resid = grad + norm_back(grad_second, unit, st["factors"][1], vecs[1:2, :])
    low = grad_resid.astype(BF)
    ct["attn"][...] = low
    shift_attn = total_rows(low.astype(F32))
    proj, gproj, gmix, scores = st["proj"], ct["proj"], work["mixed"], work["scores"]
    for t in range(2):
        gmix[t] = nn(low, w[0 : dm.width, t * dm.o_up + dm.o_out : t * dm.o_up + dm.o_ext])
    for i, t, rows, c in dm.cells():
        values = proj[t, rows, 2 * half + c : 2 * half + c + HD].astype(BF)
        gm = gmix[t, rows, c : c + HD].astype(BF)
        scores[i] = nt(gm, values)
        gproj[t, rows, 2 * half + c : 2 * half + c + HD] = tn(st["probs"][i].astype(BF), gm)
    probs, gp = st["probs"][...], scores[...]
    scores[...] = probs * (gp - jnp.sum(gp * probs, axis=-1, keepdims=True)) * SCALE
    for i, t, rows, c in dm.cells():
        query = proj[t, rows, c : c + HD].astype(BF)
        keys = proj[t, rows, half + c : half + c + HD].astype(BF)
        gs = scores[i].astype(BF)
        gproj[t, rows, c : c + HD] = nn(gs, keys)
        gproj[t, rows, half + c : half + c + HD] = tn(gs, query)
    grad_first = None
    for t in range(2):
        ct["vecs"][6:7, t * half : (t + 1) * half] = total_rows(gproj[t, :, 0:half])
        ct["vecs"][7:8, t * half : (t + 1) * half] = total_rows(gproj[t, :, 2 * half :])
        part = nt(gproj[t].astype(BF), w[0 : dm.width, t * dm.o_up : t * dm.o_up + 3 * half])
        grad_first = part if grad_first is None else grad_first + part
    unit = st["unit_one"][...]
    gain_one, shift_one = total_rows(grad_first * unit), total_rows(grad_first)
    for i, v in enumerate((gain_one, gain_two, shift_one, shift_attn, shift_two, shift_branch)):
        ct["vecs"][i : i + 1, :] = v
    return grad_resid + norm_back(grad_first, unit, st["factors"][0], vecs[0:1, :])


def parameter_grads(dm, st, ct, grads, slots):
    half, fh = dm.half, dm.fh
    block = dm.width // dm.shards

    def keep(t, column, value):
        for f in range(dm.shards):
            rows = value[f * block : (f + 1) * block].astype(BF)
            grads[slots[t][f], :, column : column + value.shape[1]] = rows

    down = tn(ct["branch"][...], st["active"][...])
    up = tn(st["second"][...], ct["hidden"][...])
    for t in range(2):
        keep(t, dm.o_down, down[:, t * fh : (t + 1) * fh])
        keep(t, dm.o_up, up[:, t * fh : (t + 1) * fh])
        keep(t, dm.o_out, tn(ct["attn"][...], st["mixed"][t].astype(BF)))
        keep(t, 0, tn(st["first"][...], ct["proj"][t].astype(BF)))
    own_first = lax.axis_index("tensor") == 0
    plain = ct["vecs"][0:6, :]
    turned = jnp.concatenate([plain[:, half:], plain[:, 0:half]], axis=1)
    plain = jnp.where(own_first, plain, turned)
    share, up_share = half // dm.shards, fh // dm.shards
    per = fh // dm.width
    for t in range(2):
        stack = jnp.concatenate([plain, ct["vecs"][6:8, :]], axis=0)[:, t * half : (t + 1) * half]
        up = jnp.concatenate([ct["vecs"][8 + t * per + j : 9 + t * per + j, :] for j in range(per)], axis=1)
        for f in range(dm.shards):
            piece = jnp.concatenate([stack[:, f * share : (f + 1) * share], jnp.zeros((8, EXT - share), F32)], axis=1)
            up_piece = up[:, f * up_share : (f + 1) * up_share]
            up_piece = jnp.concatenate([up_piece, jnp.zeros((1, EXT - up_share), F32)], axis=1)
            piece = jnp.concatenate([piece, up_piece, jnp.zeros((block - 9, EXT), F32)], axis=0)
            grads[slots[t][f], :, dm.o_ext : dm.o_up] = piece.astype(BF)


def spread(dm, ref, get):
    pad = jnp.zeros((ROW_STEP - dm.seq, dm.width), F32)
    for m in range(2):
        ref[m * ROW_STEP : m * ROW_STEP + dm.seq, :] = get(m)
        ref[m * ROW_STEP + dm.seq : (m + 1) * ROW_STEP, :] = pad


def image(dm, value, m):
    return value[m * ROW_STEP : m * ROW_STEP + dm.seq, :]


def named(shapes, refs):
    return dict(zip(shapes, refs)), refs[len(shapes) :]


def padded_images(dm, ref, out, rows, raw, sem):
    copy = pltpu.make_async_copy(ref, raw, sem.at[0])
    copy.start()
    rows[dm.seq : 96, :] = jnp.zeros((96 - dm.seq, dm.width), F32)
    copy.wait()
    value = raw[...].astype(F32)
    for m in range(2):
        rows[0 : dm.seq, :] = value[:, m, :]
        out[m] = rows[...].astype(BF)


def kernel_tokens(dm, tokens, out, rows, raw, sem):
    padded_images(dm, tokens, out, rows, raw, sem)


def kernel_cotangents(dm, count_ref, out_grad, out, rows, raw, sem):
    live = [live_of(count_ref, m) for m in range(2)]
    out[2, 0:16, :] = jnp.concatenate(
        [jnp.full((1, dm.width), v, F32) for v in live] + [jnp.zeros((14, dm.width), F32)], axis=0
    ).astype(BF)
    padded_images(dm, out_grad, out, rows, raw, sem)


def kernel_first(dm, layout, ring, images, cotangents, *refs):
    pieces, refs = refs[:-7], refs[-7:]
    w, out, proj, probs, mixed, rows, sems = refs
    st = dict(proj=proj, probs=probs, mixed=mixed)
    block = dm.width // dm.shards
    early, late, owners = [], [], {}
    if ring:
        place = picked(RING_PLACE, lax.axis_index("fsdp"))
        sign = 1 - 2 * lax.axis_index("tensor")
    for n, (t, array, row, offset) in enumerate(layout):
        if ring:
            key = offset % dm.shards
            if key not in owners:
                there = lax.rem(place + sign * key + 2 * dm.shards, dm.shards)
                owners[key] = pl.multiple_of(picked(GRID_RING, there) * block, 16)
            where = pl.ds(owners[key], block)
        else:
            where = pl.ds(offset * block, block)
        cuts = ((0, dm.o_up, t * dm.o_up), (dm.o_up, dm.fh, dm.w_up + t * dm.fh), (dm.o_down, dm.fh, dm.w_down + t * dm.fh))
        for j, (start, columns, target) in enumerate(cuts):
            source = pieces[array].at[pl.ds(row, block), pl.ds(start, columns)]
            copy = pltpu.make_async_copy(source, w.at[where, pl.ds(target, columns)], sems.at[j, n])
            (late if j else early).append(copy)
    for copy in early + late:
        copy.start()
    for m in range(2):
        columns = slice(m * dm.o_up, m * dm.o_up + dm.width)
        w[dm.o_image : dm.o_grad, columns] = images[m]
        w[dm.o_grad : dm.w_rows, columns] = cotangents[m]
        rows[m * ROW_STEP : (m + 1) * ROW_STEP, :] = images[m].astype(F32)[0:ROW_STEP]
    for copy in early:
        copy.wait()
    extra = [
        [w[f * block : f * block + 16, t * dm.o_up + dm.o_ext : (t + 1) * dm.o_up].astype(F32) for f in range(dm.shards)]
        for t in range(2)
    ]
    share, up_share = dm.half // dm.shards, dm.fh // dm.shards
    small = [
        jnp.concatenate([v[0:8, 0:share] for v in extra[t]], axis=1) for t in range(2)
    ]
    own_first = lax.axis_index("tensor") == 0
    straight = jnp.concatenate(small, axis=1)
    turned = jnp.concatenate(small[::-1], axis=1)
    vecs = [jnp.where(own_first, straight, turned)[0:6], straight[6:8]]
    per = dm.fh // dm.width
    for t in range(2):
        up = jnp.concatenate([v[8:9, 0:up_share] for v in extra[t]], axis=1)
        vecs += [up[:, j * dm.width : (j + 1) * dm.width] for j in range(per)]
    vecs.append(cotangents[2, 0:16, :].astype(F32)[0:2])
    vecs.append(jnp.zeros((6 - 2 * per, dm.width), F32))
    vecs = jnp.concatenate(vecs, axis=0)
    w[dm.o_vecs : dm.o_image, 0 : dm.width] = vecs.astype(BF)
    used = lax.axis_index("section") == 0

    @pl.when(used)
    def _():
        rows[...] = forward_attention(dm, rows[...], w, vecs, st, False)

    for copy in late:
        copy.wait()

    @pl.when(used)
    def _():
        output = forward_mlp(dm, rows[...], w, vecs, st, False)
        for m in range(2):
            out[m, 0] = image(dm, output, m).astype(BF)


def vectors_of(dm, w):
    return w[dm.o_vecs : dm.o_image, 0 : dm.width].astype(F32)


def live_of(count_ref, m):
    return (lax.axis_index("tensor") < count_ref[0, m]).astype(F32)


def ring_slots(dm, ring):
    if not ring:
        return [range(t * dm.shards, (t + 1) * dm.shards) for t in range(2)]
    place = picked(RING_PLACE, lax.axis_index("fsdp"))
    found = [[], []]
    for p in RING_PLACE:
        ahead = jnp.where(lax.axis_index("tensor") == 0, p - place, place - p)
        ahead = lax.rem(ahead + dm.shards, dm.shards)
        found[0].append(picked(KEPT_OWN, ahead))
        found[1].append(picked(KEPT_OTHER, ahead))
    return found


def kernel_second(dm, h1, w, acts, grad_in, *refs):
    st, refs = named(dm.state_shapes(), refs)
    ct, refs = named(dm.cotangent_shapes(), refs)
    work, _ = named(dm.work_shapes(), refs)
    rows = work["rows"]
    last = lax.axis_index("section") != 0

    def take(start):
        for m in range(2):
            value = w[start : start + 96, m * dm.o_up : m * dm.o_up + dm.width].astype(F32)
            rows[m * ROW_STEP : (m + 1) * ROW_STEP, :] = value[0:ROW_STEP]

    @pl.when(jnp.logical_not(last))
    def _():
        take(dm.o_image)

    @pl.when(last)
    def _():
        spread(dm, rows, lambda m: h1[m, 0].astype(F32))

    vecs = vectors_of(dm, w)
    output = forward_mlp(dm, forward_attention(dm, rows[...], w, vecs, st, True), w, vecs, st, True)
    for m in range(2):
        acts[m, 0] = (image(dm, output, m) * vecs[12 + m : 13 + m]).astype(BF)

    @pl.when(last)
    def _():
        take(dm.o_grad)
        for m in range(2):
            rows[m * ROW_STEP : (m + 1) * ROW_STEP, :] = (
                rows[m * ROW_STEP : (m + 1) * ROW_STEP, :] * vecs[12 + m : 13 + m]
            )
        grad = layer_backward(dm, rows[...], w, vecs, st, ct, work)
        for m in range(2):
            grad_in[m, 0] = image(dm, grad, m).astype(BF)


def kernel_third(dm, ring, incoming, w, own, *refs):
    st, refs = named(dm.state_shapes(), refs)
    given, refs = named(dm.cotangent_shapes(), refs)
    grad_in, grads, *refs = refs
    ct, refs = named(dm.cotangent_shapes(), refs)
    work, _ = named(dm.work_shapes(), refs)
    rows = work["rows"]
    last = lax.axis_index("section") != 0

    @pl.when(jnp.logical_not(last))
    def _():
        spread(dm, rows, lambda m: incoming[m, 0].astype(F32))
        grad = layer_backward(dm, rows[...], w, vectors_of(dm, w), st, ct, work)
        for m in range(2):
            grad_in[m, 0] = image(dm, grad, m).astype(BF)

    @pl.when(last)
    def _():
        grad_in[...] = own[...]
        for name in ct:
            ct[name][...] = given[name][...]

    parameter_grads(dm, st, ct, grads, ring_slots(dm, ring))


def kernel_unpack(dm, *refs):
    terms, (g_qkv, g_out, g_up, g_down, g_head, g_upb, g_gain, g_shift) = refs[:-8], refs[-8:]
    half, fh = dm.half, dm.fh

    def total(rows, lo, count):
        return sum(ref[rows, lo : lo + count].astype(F32) for ref in terms)

    every = slice(None)
    for k in range(3):
        g_qkv[k] = total(every, k * half, half)
    g_out[...] = total(every, dm.o_out, half)
    g_up[...] = total(every, dm.o_up, fh)
    g_down[...] = total(every, dm.o_down, fh)
    ext = total(slice(0, 16), dm.o_ext, EXT)
    share, up_share = half // dm.shards, fh // dm.shards
    g_gain[0] = ext[0:2, 0:share]
    g_shift[0] = ext[2:6, 0:share]
    g_head[0] = ext[6:8, 0:share]
    g_upb[...] = ext[8:9, 0:up_share]


VM = pl.BlockSpec(memory_space=pltpu.VMEM)
AN = pl.BlockSpec(memory_space=pl.ANY)
SM = pl.BlockSpec(memory_space=pltpu.SMEM)


def call(kernel, ins, outs, args, scratch=(), limit=16):
    return pl.pallas_call(
        kernel,
        in_specs=ins,
        out_specs=[VM] * len(outs),
        out_shape=[jax.ShapeDtypeStruct(s, d) for s, d in outs],
        scratch_shapes=list(scratch),
        compiler_params=pltpu.CompilerParams(vmem_limit_bytes=limit * 2**20),
    )(*args)


def onward(value, cycle):
    count = len(cycle)
    route = []
    for i in range(count):
        route.append((cycle[i], cycle[(i + 1) % count]))
        route.append((count + cycle[i], count + cycle[(i - 1) % count]))
    return lax.ppermute(value, ("tensor", "fsdp"), route)


def gather_ring(block, images, cycle, swap):
    far = len(cycle) // 2
    own, other = [block], [lax.ppermute(block, "tensor", swap)]
    for step in range(far):
        own.append(onward(own[-1], cycle))
        if step + 1 < far:
            other.append(onward(other[-1], cycle))
    found, places = own + other, [(0, -s) for s in range(far + 1)] + [(1, -s) for s in range(far)]
    for t, values in ((1, own), (0, other)):
        for step in range(1, len(values)):
            value = values[step]
            if t == 1 and step < far and step % 2 == 1:
                n = step // 2
                value, ready = lax.optimization_barrier((value, images[n]))
                images = images[:n] + [ready] + images[n + 1 :]
            found.append(lax.ppermute(value, "tensor", swap))
            places.append((t, step))
    layout = [(t, i, 0, offset) for i, (t, offset) in enumerate(places)]
    return found, layout, images


def reduce_ring(blocks, outputs, cycle, swap):
    count = len(cycle)
    early = 2
    first = lax.ppermute(blocks[count : count + early], "tensor", swap)

    def part(i, *more):
        given = first[i] if i < early else later[i - early]
        return sum(v.astype(F32) for v in (blocks[i], given) + more).astype(BF)

    def after(value, sent):
        return lax.optimization_barrier((value, sent))[0]

    sent = part(0)
    own = onward(sent, cycle)
    later = lax.ppermute(after(blocks[count + early :], sent), "tensor", swap)
    sent = part(1)
    other = onward(sent, cycle)
    for i in range(2, count, 2):
        sent = part(i, after(own, sent))
        own = onward(sent, cycle)
        if i + 1 < count - 1:
            sent = part(i + 1, after(other, sent))
            other = onward(sent, cycle)
    other = lax.ppermute(other, "tensor", swap)
    outputs = after(outputs, sent)
    return (blocks[count - 1], later[count - 1 - early], own, other), outputs


def per_device(tokens, out_grad, image_count, w_qkv, w_out, w_up, w_down, head_bias, up_bias, gains, shifts):
    seq, width = tokens.shape[2:]
    shards = lax.axis_size("fsdp")
    ring = shards == len(GRID_RING)
    hidden = w_up.shape[2] * 2
    dm = Dims(seq, width, hidden, len(GRID_RING))
    block = width // dm.shards
    swap = [(0, 1), (1, 0)]
    vectors = (head_bias, up_bias, gains, shifts)
    raw = [jnp.transpose(v[:, 0], (1, 0, 2)) for v in (tokens, out_grad)]
    space = [pltpu.VMEM((96, width), F32), pltpu.VMEM((seq, 2, width), BF), pltpu.SemaphoreType.DMA((1,))]
    images = [
        call(functools.partial(kernel_tokens, dm), [AN], [((2, 96, width), BF)], raw[:1], space)[0],
        call(
            functools.partial(kernel_cotangents, dm),
            [SM, AN],
            [((3, 96, width), BF)],
            (image_count.T, raw[1]),
            space,
        )[0],
    ]
    if ring:
        places = [(w_qkv[0, :, k], 0, k * dm.half) for k in range(3)]
        places += [(w_out[0].T, 0, dm.o_out), (w_up[0], 0, dm.o_up), (w_down[0].T, 0, dm.o_down)]
        places += [(v, r, dm.o_ext) for v, r in ((gains[0], 0), (shifts[0], 2), (head_bias[0], 6), (up_bias, 8))]
        packed = sum(
            jnp.pad(v, ((r, block - r - v.shape[0]), (c, dm.packed - c - v.shape[1]))) for v, r, c in places
        )
        found, layout, images = gather_ring(packed, images, GRID_RING, swap)
    else:
        rows = jnp.concatenate([w_qkv[0].reshape(w_qkv.shape[1], -1), w_out[0].T, w_up[0], w_down[0].T], axis=1)
        rows = lax.all_gather(rows, "fsdp", axis=0, tiled=True)
        front = dm.o_ext
        small = jnp.concatenate([gains[0], shifts[0], head_bias[0]], axis=0)
        small = lax.all_gather(small, "fsdp", axis=1, tiled=True)
        up = lax.all_gather(up_bias, "fsdp", axis=1, tiled=True)
        small = jnp.moveaxis(small.reshape(8, dm.shards, -1), 1, 0)
        ext = jnp.concatenate(
            [
                jnp.pad(small, ((0, 0), (0, 0), (0, EXT - small.shape[2]))),
                jnp.pad(
                    up.reshape(dm.shards, 1, -1), ((0, 0), (0, block - 9), (0, EXT - up.shape[1] // dm.shards))
                ),
            ],
            axis=1,
        )
        rows = jnp.concatenate([rows[:, :front], ext.reshape(width, EXT), rows[:, front:]], axis=1)
        found = [rows, lax.ppermute(rows, "tensor", swap)]
        layout = [(t, t, i * block, i) for t in range(2) for i in range(dm.shards)]
    states = dm.state_shapes()
    cotangents = dm.cotangent_shapes()
    shape = tokens.shape
    buffers = lambda shapes: [pltpu.VMEM(*v) for v in shapes]
    work = buffers(dm.work_shapes().values())
    w, low0 = call(
        functools.partial(kernel_first, dm, layout, ring),
        [VM, VM] + [AN] * len(found),
        [((dm.w_rows, 2 * dm.packed), BF), (shape, BF)],
        (*images, *found),
        scratch=buffers([states["proj"], states["probs"], states["mixed"], ((dm.rows, width), F32)])
        + [pltpu.SemaphoreType.DMA((3, len(layout)))],
    )
    h1 = lax.ppermute(low0, "section", [(0, 1)])
    kept = list(states.values()) + list(cotangents.values())
    acts, grad1, *kept = call(
        functools.partial(kernel_second, dm),
        [VM] * 2,
        [(shape, BF), (shape, BF)] + kept,
        (h1, w),
        scratch=work,
    )
    incoming = lax.ppermute(grad1, "section", [(1, 0)])
    in_grads, blocks = call(
        functools.partial(kernel_third, dm, ring),
        [VM] * (3 + len(kept)),
        [(shape, BF), ((2 * dm.shards, block, dm.packed), BF)],
        (incoming, w, grad1) + tuple(kept),
        scratch=buffers(cotangents.values()) + work,
    )
    if ring:
        terms, (acts, in_grads) = reduce_ring(blocks, (acts, in_grads), GRID_RING, swap)
        shapes = [(3, block, dm.half), (block, dm.half), (block, dm.fh), (block, dm.fh)] + [v.shape for v in vectors]
        g_qkv, g_out, g_up, g_down, *small = call(
            functools.partial(kernel_unpack, dm), [VM] * len(terms), [(v, F32) for v in shapes], terms
        )
        grads = [jnp.transpose(g_qkv, (1, 0, 2))[None], g_out.T[None], g_up[None], g_down.T[None], *small]
    else:
        half = dm.half
        mine = blocks[: dm.shards].astype(F32)
        mine += lax.ppermute(blocks[dm.shards :], "tensor", swap).astype(F32)
        mine = mine.reshape(width, dm.packed)
        body = jnp.concatenate([mine[:, : dm.o_ext], mine[:, dm.o_up :]], axis=1)
        body = lax.psum_scatter(body, "fsdp", scatter_dimension=0, tiled=True)
        up_at, down_at = dm.o_ext, dm.o_ext + dm.fh
        share, up_share = half // dm.shards, dm.fh // dm.shards
        ext = mine[:, dm.o_ext : dm.o_up].reshape(dm.shards, block, EXT)
        small = jnp.moveaxis(ext[:, 0:8, 0:share], 0, 1).reshape(8, half)
        small = lax.psum_scatter(small, "fsdp", scatter_dimension=1, tiled=True)
        up = lax.psum_scatter(ext[:, 8, 0:up_share].reshape(-1), "fsdp", scatter_dimension=0, tiled=True)
        grads = [
            body[:, : 3 * half].reshape(w_qkv.shape),
            body[:, dm.o_out : up_at].T[None],
            body[:, up_at : down_at][None],
            body[:, down_at:].T[None],
            small[6:8][None],
            up[None],
            small[0:2][None],
            small[2:6][None],
        ]
    return (acts[None], in_grads[None], *grads)


def solution(mesh):
    both = ("tensor", "fsdp")
    params = (
        P("section", "fsdp", None, "tensor"),
        P("section", "tensor", "fsdp"),
        P("section", "fsdp", "tensor"),
        P("section", "tensor", "fsdp"),
        P("section", None, both),
        P("section", both),
        P("section", None, both),
        P("section", None, both),
    )
    images = P(None, ("fsdp", "tensor"), None, None)
    layered = P("section", None, ("fsdp", "tensor"), None, None)
    return jax.shard_map(
        per_device,
        mesh=mesh,
        in_specs=(images, images, P(None, "fsdp")) + params,
        out_specs=(layered, layered) + params,
        check_vma=False,
    )
```
